32 devices in a mesh: axial: 4 (over y, x), cross: 8 (over z, core).
Axes of the slice: x: 2, y: 2, z: 4, core: 2. Of those that a mesh axis runs over, the one named last changes fastest.
Arguments:
- force: float32 [4, 8, 8, 3, 128], P('axial', 'cross'), may hold values from -6 to 6
- self_drag: float32 [4, 8, 8, 128], P('axial', 'cross'), may hold values from 0.5 to 4
- tiles: bfloat16 [4, 8, 8, 8, 128, 128], P('axial', 'cross'), may hold values from -0.1875 to 0.1875
- tile_ids: int32 [4, 8, 8, 8], P('axial', 'cross'), may hold values from 8 to 63, as said below
- mig_rows: int32 [4, 8, 2, 64], P('axial', 'cross'), may hold values from 0 to 1023, as said below
- mig_count: int32 [4, 8, 2], P('axial', 'cross'), may hold values from 0 to 64, as said below
Outputs:
- velocity: float32 [4, 8, 8, 3, 128], P('axial', 'cross')
- residual: float32 [4, 8, 8, 3, 128], P('axial', 'cross')
- arrivals: float32 [4, 8, 3, 128], P('axial', 'cross')
The draws below stay inside these ranges and needn't reach their ends.
Inputs may be any that keep to these rules, and one draw needn't show every extreme that they name: `tile_ids`: each entry is p * 8 + q with p one of 1, 3, 4, 5, 7 and q below 8; the first five tiles of every block name the five values of p. `mig_rows`: the 128 entries of one device are distinct beads. `mig_count`: the lowest slab sends nothing to the lower side and the highest nothing to the upper side; in every axial group one slab sends 64 beads to both sides.
All inputs are finite; a program needn't handle non-finite values.
Results may differ from the reference program's by a relative error of at most 0.024.
Values may be sent and summed in bfloat16 or wider, within the bound.
A program may use at most 64 MiB of HBM per device.

```python
import math
import jax
import jax.numpy as jnp
from jax import lax

BLOCK = 128
TILES = 8
BLK_DEV = 8
SLOT = 64
ITERS = 3
AXIAL_GROUPS = 4
SLABS = 8


def draw_tile_ids(key, part):
    first, second, third = jax.random.split(key, 3)
    shape = (AXIAL_GROUPS, SLABS, BLK_DEV, TILES)
    offset = jax.random.randint(first, (AXIAL_GROUPS, SLABS, BLK_DEV, 1), 0, 5)
    spare = jax.random.randint(second, shape, 0, 5)
    column = lax.broadcasted_iota(jnp.int32, shape, 3)
    region = jnp.where(column < 5, (offset + column) % 5, spare)
    table = jnp.array([4, 1, 7, 3, 5], dtype=jnp.int32)
    place = jnp.take(table, region)
    member = jax.random.randint(third, shape, 0, BLK_DEV)
    return (place * BLK_DEV + member).astype(jnp.int32)


def draw_mig_rows(key, part):
    keys = jax.random.split(jax.random.fold_in(key, 11), AXIAL_GROUPS * SLABS)

    def one_device(device_key):
        return jax.random.permutation(device_key, BLK_DEV * BLOCK)[:2 * SLOT]
    chosen = jax.vmap(one_device)(keys)
    return chosen.reshape(AXIAL_GROUPS, SLABS, 2, SLOT).astype(jnp.int32)


def draw_mig_count(key, part):
    first, second = jax.random.split(jax.random.fold_in(key, 23), 2)
    shape = (AXIAL_GROUPS, SLABS, 2)
    counts = jax.random.randint(first, shape, (SLOT + 2) // 3, SLOT + 1)
    target = jax.random.randint(second, (AXIAL_GROUPS, 1, 1), 1, SLABS - 1)
    slab = lax.broadcasted_iota(jnp.int32, shape, 1)
    side = lax.broadcasted_iota(jnp.int32, shape, 2)
    counts = jnp.where(slab == target, SLOT, counts)
    edge = jnp.logical_or(jnp.logical_and(side == 0, slab == 0), jnp.logical_and(side == 1, slab == SLABS - 1))
    return jnp.where(edge, 0, counts).astype(jnp.int32)


def level_of(rng, shape, cuts, least, largest):
    def one(position, blocks):
        heights = jax.random.uniform(jax.random.fold_in(jax.random.fold_in(rng, 6), position), (blocks,), jnp.float32, least / len(cuts), largest / len(cuts))
        return jnp.repeat(jnp.exp(heights), shape[position] // blocks).reshape((-1,) + (1,) * (len(shape) - position - 1))

    gain = one(*cuts[0])
    for cut in cuts[1:]:
        gain = gain * one(*cut)
    return gain


def bell_draw(rng, shape, deviation, reach, cuts=(), kind=jnp.bfloat16):
    level = level_of(rng, shape, cuts, -0.22, 0.18) if cuts else 1.0
    values = jax.random.normal(rng, shape, jnp.float32) * deviation * level
    return jnp.minimum(jnp.maximum(values, -reach), reach).astype(kind)


def setup_inputs(seed: int = 0) -> dict:
    key_of = jax.random.split(jax.random.key(seed), 7)
    return {
        "force": bell_draw(key_of[0], (AXIAL_GROUPS, SLABS, BLK_DEV, 3, BLOCK), 1.0, 6.0, ((0, 4), (1, 8)), jnp.float32),
        "self_drag": jnp.clip(jnp.exp(math.log(4.0) - 2.0794415 * jax.random.uniform(key_of[1], (AXIAL_GROUPS, SLABS, BLK_DEV, BLOCK), jnp.float32) ** level_of(key_of[1], (AXIAL_GROUPS, SLABS, BLK_DEV, BLOCK), ((0, 4), (1, 8)), -0.2, 0.2)), 0.5, 4.0),
        "tiles": bell_draw(key_of[2], (AXIAL_GROUPS, SLABS, BLK_DEV, TILES, BLOCK, BLOCK), (TILES * BLOCK) ** -0.5, 0.1875, ((0, 4), (1, 8))),
        "tile_ids": draw_tile_ids(jax.random.fold_in(key_of[6], 71), 0),
        "mig_rows": draw_mig_rows(jax.random.fold_in(key_of[6], 71), 0),
        "mig_count": draw_mig_count(jax.random.fold_in(key_of[6], 71), 0),
    }


def extended_list(field):
    blanks = jnp.zeros_like(field)
    below_axial = jnp.roll(field, 1, axis=0)
    above_axial = jnp.roll(field, -1, axis=0)
    below_cross = jnp.concatenate([blanks[:, :1], field[:, :-1]], axis=1)
    above_cross = jnp.concatenate([field[:, 1:], blanks[:, :1]], axis=1)
    stacked = jnp.stack([blanks, below_axial, blanks, below_cross, field, above_cross, blanks, above_axial, blanks], axis=2)
    return stacked.reshape(AXIAL_GROUPS * SLABS, 9 * BLK_DEV, 3, BLOCK)


def device_product(operands):
    extended, tile_block, id_block = operands
    picked = extended[id_block].astype(jnp.float32)
    tile_wide = tile_block.astype(jnp.float32)
    coupled = jnp.einsum("bkij,bkcj->bci", tile_wide, picked).astype(jnp.bfloat16)
    spread = jnp.einsum("bkij,bci->bkcj", tile_wide, coupled.astype(jnp.float32))
    return jax.ops.segment_sum(spread.reshape(-1, 3, BLOCK), id_block.reshape(-1), num_segments=9 * BLK_DEV)


def apply_operator(direction, self_drag, tiles, tile_ids):
    lowered = direction.astype(jnp.bfloat16)
    extended = extended_list(lowered)
    flat_tiles = tiles.reshape(AXIAL_GROUPS * SLABS, BLK_DEV, TILES, BLOCK, BLOCK)
    flat_ids = tile_ids.reshape(AXIAL_GROUPS * SLABS, BLK_DEV, TILES)
    returned = lax.map(device_product, (extended, flat_tiles, flat_ids))
    returned = returned.reshape(AXIAL_GROUPS, SLABS, 9, BLK_DEV, 3, BLOCK)
    zeros_slab = jnp.zeros_like(returned[:, :1, 0])
    total = returned[:, :, 4]
    total = total + jnp.roll(returned[:, :, 1], -1, axis=0)
    total = total + jnp.roll(returned[:, :, 7], 1, axis=0)
    total = total + jnp.concatenate([returned[:, 1:, 3], zeros_slab], axis=1)
    total = total + jnp.concatenate([zeros_slab, returned[:, :-1, 5]], axis=1)
    return self_drag[:, :, :, None, :] * direction + total


def pick_rows(flat, rows):
    return flat[:, rows.reshape(-1)]


def reference(force, self_drag, tiles, tile_ids, mig_rows, mig_count):
    velocity = jnp.zeros_like(force)
    residual = force
    direction = force
    norm_now = jnp.sum(residual * residual)
    for sweep in range(ITERS):
        image = apply_operator(direction, self_drag, tiles, tile_ids)
        alpha = norm_now / jnp.sum(direction * image)
        velocity = velocity + alpha * direction
        residual = residual - alpha * image
        norm_next = jnp.sum(residual * residual)
        direction = residual + (norm_next / norm_now) * direction
        norm_now = norm_next
    flat = jnp.swapaxes(velocity, 2, 3).reshape(AXIAL_GROUPS, SLABS, 3, BLK_DEV * BLOCK)
    picked = jax.vmap(jax.vmap(pick_rows))(flat, mig_rows)
    picked = picked.reshape(AXIAL_GROUPS, SLABS, 3, 2, SLOT)
    live = jnp.arange(SLOT, dtype=jnp.int32)[None, None, None, None, :] < mig_count[:, :, None, :, None]
    sent = jnp.where(live, picked, jnp.zeros_like(picked))
    blank = jnp.zeros_like(sent[:, :1, :, 0])
    from_lower = jnp.concatenate([blank, sent[:, :-1, :, 1]], axis=1)
    from_upper = jnp.concatenate([sent[:, 1:, :, 0], blank], axis=1)
    arrivals = jnp.concatenate([from_lower, from_upper], axis=3)
    return velocity, residual, arrivals
```

```python
import functools

import jax
import jax.numpy as jnp
from jax import lax
from jax.experimental import pallas as pl
from jax.experimental.pallas import tpu as pltpu
from jax.sharding import PartitionSpec as P

ITERS = 3
MESH = pl.DeviceIdType.MESH
PLACES = (1, 3, 5, 7)
CENTRE = 4
F32 = jnp.float32
BF16 = jnp.bfloat16


def chunks(field):
    return [field[:, c * 128:(c + 1) * 128] for c in range(3)]


def kernel(
    n_ax, n_cr,
    ids_ref, count_ref, force_ref, drag_ref, tiles_ref, rows_ref,
    vel_ref, res_ref, arr_ref,
    tile_buf, ext, spread, own, halo, ret_out, ret_in, part_ax, part_cr, mig, rows_out, rows_in,
    tile_sem, halo_send, halo_recv, ret_send, ret_recv, rows_send, rows_recv,
    ax_send, ax_recv, cr_send, cr_recv,
):
    blocks, count, width = tiles_ref.shape[0], tiles_ref.shape[1], tiles_ref.shape[2]
    pairs = blocks * count
    slot = rows_ref.shape[1]
    me_a = lax.axis_index("axial")
    me_c = lax.axis_index("cross")

    def ax_peer(step):
        return {"axial": lax.rem(me_a + step, n_ax)}

    def cr_peer(step):
        return {"cross": lax.rem(me_c + step, n_cr)}

    device = (ax_peer(n_ax - 1), cr_peer(n_cr - 1), cr_peer(1), ax_peer(1))
    exists = (None, me_c > 0, me_c + 1 < n_cr, None)

    def guarded(d, act):
        if exists[d] is None:
            act()
        else:
            pl.when(exists[d])(act)

    def neighbour(src, dst, send, recv, d, back):
        s = d if back else 3 - d
        return pltpu.make_async_remote_copy(
            src_ref=src, dst_ref=dst.at[s], send_sem=send.at[d], recv_sem=recv.at[s],
            device_id=device[d], device_id_type=MESH,
        )

    def halo_copy(stage, d, back=False):
        return neighbour(own.at[stage], halo.at[stage], halo_send.at[stage], halo_recv.at[stage], d, back)

    def ret_copy(it, d, back=False):
        src = ret_out.at[it, pl.ds(PLACES[d] * blocks, blocks)]
        return neighbour(src, ret_in.at[it], ret_send.at[it], ret_recv.at[it], d, back)

    def rows_copy(d, back=False):
        return neighbour(rows_out.at[d], rows_in, rows_send, rows_recv, d, back)

    def ax_copy(it, step):
        return pltpu.make_async_remote_copy(
            src_ref=part_ax.at[it, me_a], dst_ref=part_ax.at[it, me_a],
            send_sem=ax_send.at[it, step], recv_sem=ax_recv.at[it, step],
            device_id=ax_peer(step), device_id_type=MESH,
        )

    def cr_copy(it, step):
        return pltpu.make_async_remote_copy(
            src_ref=part_cr.at[it, me_c], dst_ref=part_cr.at[it, me_c],
            send_sem=cr_send.at[it, step], recv_sem=cr_recv.at[it, step],
            device_id=cr_peer(step), device_id_type=MESH,
        )

    barrier = pltpu.get_barrier_semaphore()
    for step in range(1, n_ax):
        pl.semaphore_signal(barrier, inc=1, device_id=ax_peer(step), device_id_type=MESH)
    for step in range(1, n_cr):
        pl.semaphore_signal(barrier, inc=1, device_id=cr_peer(step), device_id_type=MESH)

    load = pltpu.make_async_copy(tiles_ref, tile_buf, tile_sem)
    load.start()

    force = jnp.concatenate([force_ref[c] for c in range(3)], axis=1)
    own[0] = force
    lane = lax.broadcasted_iota(jnp.int32, (1, 128), 1)
    mig[0:2, 0:slot] = rows_ref[...]
    listed = mig[...]
    turned = pltpu.roll(listed, 64, 1)
    rows_out[1] = jnp.where((lane < slot) & (lane < count_ref[0]), listed[0:1], -1)
    rows_out[2] = jnp.where((lane >= 64) & (lane - 64 < count_ref[1]), turned[1:2], -1)

    for d in (1, 2):
        @pl.when(jnp.logical_not(exists[d]))
        def _():
            for stage in range(ITERS):
                halo[stage, d] = jnp.zeros((blocks, 3 * width), F32)
                ret_in[stage, d] = jnp.zeros((blocks, 3 * width), F32)
            rows_in[d] = jnp.full((1, 128), -1, jnp.int32)

    pl.semaphore_wait(barrier, n_ax - 1 + n_cr - 1)

    for d in range(4):
        guarded(d, lambda d=d: halo_copy(0, d).start())
    for d in (1, 2):
        guarded(d, lambda d=d: rows_copy(d).start())

    ext[...] = jnp.zeros(ext.shape, F32)
    wide = lax.broadcasted_iota(jnp.int32, (1, 2 * pairs), 1)
    listed_ids = jnp.zeros((1, 2 * pairs), jnp.int32)
    for n in range(pairs):
        hit = (wide == n) | (wide == n + pairs)
        listed_ids = jnp.where(hit, ids_ref[n // count, n % count], listed_ids)
    entry = lax.broadcasted_iota(jnp.int32, (8 * blocks, 2 * pairs), 0)
    selector = jnp.where(entry == listed_ids, 1.0, 0.0).astype(BF16)
    drag = drag_ref[...]
    drag3 = jnp.concatenate([drag] * 3, axis=1)

    def place(p, field):
        for c, part in enumerate(chunks(field)):
            ext[p * blocks:(p + 1) * blocks, c, :] = part

    def tile_row(b):
        return jnp.concatenate([tile_buf[b, k] for k in range(count)], axis=1)

    def total(parts):
        return jnp.sum(functools.reduce(jnp.add, parts), axis=0, keepdims=True)

    place(CENTRE, force)
    residual = force
    velocity = direction = image = None
    near = [None] * 4
    near_image = [None] * 4
    near_velocity = [None] * 4
    near_direction = [None] * 4
    track = [None] * blocks
    norm_before = energy_before = None

    for d in range(4):
        guarded(d, lambda d=d: halo_copy(0, d, True).wait_recv())
        near[d] = halo[0, d]
    load.wait()

    for it in range(ITERS):
        last = it == ITERS - 1
        if it:
            place(CENTRE, residual)
        for d in range(4):
            place(PLACES[d], near[d])
        coupled = []
        for b in range(blocks):
            picked = jnp.concatenate([ext[ids_ref[b, k]] for k in range(count)], axis=1)
            coupled.append(lax.dot_general(
                picked.astype(BF16), tile_row(b), (((1,), (1,)), ((), ())), preferred_element_type=F32,
            ))

        square = functools.reduce(jnp.add, chunks(residual * residual))
        sums = [
            jnp.sum(square, axis=0, keepdims=True),
            total([drag * square] + [c * c for c in coupled]),
        ]
        if it:
            mixed = functools.reduce(jnp.add, chunks(residual * direction))
            sums.append(total([drag * mixed] + [c * t for c, t in zip(coupled, track)]))
        else:
            sums.append(jnp.zeros((1, 128), F32))
        part_ax[it, me_a] = jnp.concatenate(sums, axis=1)
        for step in range(1, n_ax):
            ax_copy(it, step).start()

        for b in range(blocks):
            back = jnp.dot(coupled[b].astype(BF16), tile_row(b), preferred_element_type=F32)
            for k in range(count):
                spread[b * count + k] = back[:, k * width:(k + 1) * width]
        listed_spread = jnp.concatenate([spread[:, c, :] for c in range(3)], axis=1)
        high = listed_spread.astype(BF16)
        low = (listed_spread - high.astype(F32)).astype(BF16)
        ret_out[it] = jnp.dot(
            selector, jnp.concatenate([high, low], axis=0), preferred_element_type=F32
        )
        for d in range(4):
            guarded(d, lambda d=d: ret_copy(it, d).start())

        for step in range(1, n_ax):
            ax_copy(it, step).wait_recv()
        part_cr[it, me_c] = functools.reduce(jnp.add, [part_ax[it, i] for i in range(n_ax)])
        for step in range(1, n_cr):
            cr_copy(it, step).start()

        if last:
            gathered = [0.0] * 9
            for d in (1, 2):
                if it == ITERS - 1:
                    guarded(d, lambda d=d: rows_copy(d, True).wait_recv())
                rows = rows_in[d]
                fields = [near_velocity[d], near[d], near_direction[d]]
                stack = jnp.concatenate([part for f in fields for part in chunks(f)], axis=0)
                first = stack.astype(BF16)
                rest = stack - first.astype(F32)
                second = rest.astype(BF16)
                third = (rest - second.astype(F32)).astype(BF16)
                bead = lax.broadcasted_iota(jnp.int32, (width, 128), 0)
                onehot = jnp.where(bead == (rows & (width - 1)), 1.0, 0.0).astype(BF16)
                found = sum(
                    jnp.dot(piece, onehot, preferred_element_type=F32) for piece in (third, second, first)
                )
                block = lax.broadcasted_iota(jnp.int32, (blocks, 128), 0)
                mine = block == (rows >> (width.bit_length() - 1))
                for n in range(9):
                    part = jnp.where(mine, found[n * blocks:(n + 1) * blocks], 0.0)
                    gathered[n] = gathered[n] + jnp.sum(part, axis=0, keepdims=True)

        for d in range(4):
            guarded(d, lambda d=d: ret_copy(it, d, True).wait_recv())
        product = drag3 * residual + ret_out[it, CENTRE * blocks:(CENTRE + 1) * blocks]
        for d in range(4):
            product = product + ret_in[it, d]
        if not last:
            own[it + 1] = product
            for d in range(4):
                guarded(d, lambda d=d: halo_copy(it + 1, d).start())

        for step in range(1, n_cr):
            cr_copy(it, step).wait_recv()
        summed = functools.reduce(jnp.add, [part_cr[it, i] for i in range(n_cr)])
        norm, energy, cross = [jnp.sum(s, axis=1, keepdims=True) for s in chunks(summed)]
        if it:
            beta = norm / norm_before
            energy = energy + 2.0 * beta * cross + beta * beta * energy_before
        alpha = norm / energy
        norm_before, energy_before = norm, energy

        def follow(now, before):
            return now + beta * before if it else now

        image = follow(product, image)
        direction = follow(residual, direction)
        velocity = velocity + alpha * direction if it else alpha * direction
        residual = residual - alpha * image
        if last:
            break
        track = [follow(c, t) for c, t in zip(coupled, track)]
        for d in range(4):
            guarded(d, lambda d=d: halo_copy(it + 1, d, True).wait_recv())
            near_image[d] = follow(halo[it + 1, d], near_image[d])
            if d in (1, 2):
                near_direction[d] = follow(near[d], near_direction[d])
                step_v = alpha * near_direction[d]
                near_velocity[d] = near_velocity[d] + step_v if it else step_v
            near[d] = near[d] - alpha * near_image[d]

    for c in range(3):
        vel_ref[c] = chunks(velocity)[c]
        res_ref[c] = chunks(residual)[c]
    sub = lax.broadcasted_iota(jnp.int32, (8, 128), 0)
    arrived = jnp.zeros((8, 128), F32)
    for c in range(3):
        row = gathered[c] + alpha * (gathered[3 + c] + beta * gathered[6 + c])
        arrived = jnp.where(sub == c, row, arrived)
    arr_ref[...] = pltpu.roll(arrived, 64, 1)[0:3]

    for d in (1, 2):
        guarded(d, lambda d=d: rows_copy(d).wait_send())
    for it in range(ITERS):
        for d in range(4):
            guarded(d, lambda d=d: halo_copy(it, d).wait_send())
            guarded(d, lambda d=d: ret_copy(it, d).wait_send())
        for step in range(1, n_ax):
            ax_copy(it, step).wait_send()
        for step in range(1, n_cr):
            cr_copy(it, step).wait_send()


def on_device(n_ax, n_cr, force, self_drag, tiles, tile_ids, mig_rows, mig_count):
    blocks, width = force.shape[2], force.shape[4]
    count = tiles.shape[3]
    field = (blocks, 3 * width)
    vmem = pl.BlockSpec(memory_space=pltpu.VMEM)
    smem = pl.BlockSpec(memory_space=pltpu.SMEM)
    dma = pltpu.SemaphoreType.DMA
    velocity, residual, arrivals = pl.pallas_call(
        functools.partial(kernel, n_ax, n_cr),
        out_shape=(
            jax.ShapeDtypeStruct((3, blocks, width), F32),
            jax.ShapeDtypeStruct((3, blocks, width), F32),
            jax.ShapeDtypeStruct((3, 2 * mig_rows.shape[3]), F32),
        ),
        in_specs=[smem, smem, vmem, vmem, pl.BlockSpec(memory_space=pl.ANY), vmem],
        out_specs=(vmem, vmem, vmem),
        scratch_shapes=[
            pltpu.VMEM((blocks, count, width, width), BF16),
            pltpu.VMEM((8 * blocks, 8, width), F32),
            pltpu.VMEM((blocks * count, 8, width), F32),
            pltpu.VMEM((ITERS,) + field, F32),
            pltpu.VMEM((ITERS, 4) + field, F32),
            pltpu.VMEM((ITERS, 8 * blocks, 3 * width), F32),
            pltpu.VMEM((ITERS, 4) + field, F32),
            pltpu.VMEM((ITERS, n_ax, 1, 384), F32),
            pltpu.VMEM((ITERS, n_cr, 1, 384), F32),
            pltpu.VMEM((8, 128), jnp.int32),
            pltpu.VMEM((3, 1, 128), jnp.int32),
            pltpu.VMEM((3, 1, 128), jnp.int32),
            dma,
            dma((ITERS, 4)), dma((ITERS, 4)),
            dma((ITERS, 4)), dma((ITERS, 4)),
            dma((3,)), dma((3,)),
            dma((ITERS, n_ax)), dma((ITERS, n_ax)),
            dma((ITERS, n_cr)), dma((ITERS, n_cr)),
        ],
        compiler_params=pltpu.CompilerParams(
            collective_id=0, has_side_effects=True, vmem_limit_bytes=60 * 1024 * 1024
        ),
        name="cg_solve",
    )(
        tile_ids.reshape(tile_ids.shape[2:]),
        mig_count.reshape(mig_count.shape[2:]),
        jnp.swapaxes(force[0, 0], 0, 1),
        self_drag.reshape(self_drag.shape[2:]),
        tiles.reshape(tiles.shape[2:]),
        mig_rows.reshape(mig_rows.shape[2:]),
    )
    velocity, residual = jnp.swapaxes(velocity, 0, 1), jnp.swapaxes(residual, 0, 1)
    return velocity[None, None], residual[None, None], arrivals[None, None]


def solution(mesh):
    placed = (
        P("axial", "cross", None, None, None),
        P("axial", "cross", None, None),
        P("axial", "cross", None, None, None, None),
        P("axial", "cross", None, None),
        P("axial", "cross", None, None),
        P("axial", "cross", None),
    )
    return jax.shard_map(
        functools.partial(on_device, mesh.shape["axial"], mesh.shape["cross"]),
        mesh=mesh,
        in_specs=placed,
        out_specs=(
            P("axial", "cross", None, None, None),
            P("axial", "cross", None, None, None),
            P("axial", "cross", None, None),
        ),
        check_vma=False,
    )
```

```python
import functools

import jax
import jax.numpy as jnp
from jax import lax
from jax.experimental import pallas as pl
from jax.experimental.pallas import tpu as pltpu
from jax.sharding import PartitionSpec as P

ITERS = 3
MESH = pl.DeviceIdType.MESH
PLACES = (1, 3, 5, 7)
CENTRE = 4
F32 = jnp.float32
BF16 = jnp.bfloat16


def chunks(field):
    return [field[:, c * 128:(c + 1) * 128] for c in range(3)]


def kernel(
    n_ax, n_cr,
    ids_hbm, count_hbm, force_hbm, drag_hbm, tiles_ref, rows_hbm,
    vel_ref, res_ref, arr_ref,
    ids_ref, count_ref, force_ref, drag_ref, rows_ref, tile_buf, ext, spread, own, halo, ret_out, ret_in, part_ax, part_cr, mig, rows_out, rows_in,
    tile_sem, small_sem, halo_send, halo_recv, ret_send, ret_recv, rows_send, rows_recv,
    ax_send, ax_recv, cr_send, cr_recv,
):
    blocks, count, width = tiles_ref.shape[0], tiles_ref.shape[1], tiles_ref.shape[2]
    pairs = blocks * count
    slot = rows_hbm.shape[1]
    me_a = lax.axis_index("axial")
    me_c = lax.axis_index("cross")

    def ax_peer(step):
        return {"axial": lax.rem(me_a + step, n_ax)}

    def cr_peer(step):
        return {"cross": lax.rem(me_c + step, n_cr)}

    device = (ax_peer(n_ax - 1), cr_peer(n_cr - 1), cr_peer(1), ax_peer(1))
    exists = (None, me_c > 0, me_c + 1 < n_cr, None)

    def guarded(d, act):
        if exists[d] is None:
            act()
        else:
            pl.when(exists[d])(act)

    def neighbour(src, dst, send, recv, d):
        return pltpu.make_async_remote_copy(
            src_ref=src, dst_ref=dst.at[3 - d], send_sem=send, recv_sem=recv,
            device_id=device[d], device_id_type=MESH,
        )

    def halo_copy(stage, d):
        return neighbour(own.at[stage], halo.at[stage], halo_send.at[d], halo_recv.at[stage], d)

    def ret_copy(it, d):
        src = ret_out.at[it, pl.ds(PLACES[d] * blocks, blocks)]
        return neighbour(src, ret_in.at[it], ret_send.at[d], ret_recv.at[it], d)

    def rows_copy(d):
        return neighbour(rows_out.at[d], rows_in, rows_send.at[d], rows_recv.at[3 - d], d)

    def wait_for(ref, sem):
        pltpu.make_async_copy(ref, ref, sem).wait()

    inner = exists[1] & exists[2]

    def arrived_all(ref, sem):
        @pl.when(inner)
        def _():
            wait_for(ref, sem)

        @pl.when(jnp.logical_not(inner))
        def _():
            wait_for(ref.at[pl.ds(0, 3)], sem)

    def ax_copy(it, step):
        return pltpu.make_async_remote_copy(
            src_ref=part_ax.at[it, me_a], dst_ref=part_ax.at[it, me_a],
            send_sem=ax_send, recv_sem=ax_recv.at[it],
            device_id=ax_peer(step), device_id_type=MESH,
        )

    def cr_copy(it, step):
        return pltpu.make_async_remote_copy(
            src_ref=part_cr.at[it, me_c], dst_ref=part_cr.at[it, me_c],
            send_sem=cr_send, recv_sem=cr_recv.at[it],
            device_id=cr_peer(step), device_id_type=MESH,
        )

    fetched = (
        (force_hbm, force_ref), (ids_hbm, ids_ref), (count_hbm, count_ref),
        (drag_hbm, drag_ref), (rows_hbm, rows_ref),
    )
    small = [pltpu.make_async_copy(a, b, small_sem.at[n]) for n, (a, b) in enumerate(fetched)]
    for copy in small:
        copy.start()

    barrier = pltpu.get_barrier_semaphore()
    for step in range(1, n_ax):
        pl.semaphore_signal(barrier, inc=1, device_id=ax_peer(step), device_id_type=MESH)
    for step in range(1, n_cr):
        pl.semaphore_signal(barrier, inc=1, device_id=cr_peer(step), device_id_type=MESH)

    load = pltpu.make_async_copy(tiles_ref, tile_buf, tile_sem)
    load.start()
    for copy in small:
        copy.wait()

    force = jnp.concatenate([force_ref[c] for c in range(3)], axis=1)
    own[0] = force
    lane = lax.broadcasted_iota(jnp.int32, (1, 128), 1)
    mig[0:2, 0:slot] = rows_ref[...]
    listed = mig[...]
    turned = pltpu.roll(listed, 64, 1)
    rows_out[1] = jnp.where((lane < slot) & (lane < count_ref[0]), listed[0:1], -1)
    rows_out[2] = jnp.where((lane >= 64) & (lane - 64 < count_ref[1]), turned[1:2], -1)

    for d in (1, 2):
        @pl.when(jnp.logical_not(exists[d]))
        def _():
            for stage in range(ITERS):
                halo[stage, d] = jnp.zeros((blocks, 3 * width), F32)
                ret_in[stage, d] = jnp.zeros((blocks, 3 * width), F32)
            rows_in[d] = jnp.full((1, 128), -1, jnp.int32)

    pl.semaphore_wait(barrier, n_ax - 1 + n_cr - 1)

    for d in range(4):
        guarded(d, lambda d=d: halo_copy(0, d).start())
    for d in (1, 2):
        guarded(d, lambda d=d: rows_copy(d).start())

    ext[...] = jnp.zeros(ext.shape, F32)
    wide = lax.broadcasted_iota(jnp.int32, (1, 2 * pairs), 1)
    listed_ids = jnp.zeros((1, 2 * pairs), jnp.int32)
    for n in range(pairs):
        hit = (wide == n) | (wide == n + pairs)
        listed_ids = jnp.where(hit, ids_ref[n // count, n % count], listed_ids)
    entry = lax.broadcasted_iota(jnp.int32, (8 * blocks, 2 * pairs), 0)
    selector = jnp.where(entry == listed_ids, 1.0, 0.0).astype(BF16)
    drag = drag_ref[...]
    drag3 = jnp.concatenate([drag] * 3, axis=1)

    def place(p, field):
        for c, part in enumerate(chunks(field)):
            ext[p * blocks:(p + 1) * blocks, c, :] = part

    def tile_row(b):
        return jnp.concatenate([tile_buf[b, k] for k in range(count)], axis=1)

    def total(parts):
        return jnp.sum(functools.reduce(jnp.add, parts), axis=0, keepdims=True)

    place(CENTRE, force)
    residual = force
    velocity = direction = image = None
    near = [None] * 4
    near_image = [None] * 4
    near_velocity = [None] * 4
    near_direction = [None] * 4
    track = [None] * blocks
    norm_before = energy_before = None

    arrived_all(halo.at[0], halo_recv.at[0])
    for d in range(4):
        near[d] = halo[0, d]
    load.wait()

    for it in range(ITERS):
        last = it == ITERS - 1
        if it:
            place(CENTRE, residual)
        for d in range(4):
            place(PLACES[d], near[d])
        coupled = []
        for b in range(blocks):
            picked = jnp.concatenate([ext[ids_ref[b, k]] for k in range(count)], axis=1)
            coupled.append(lax.dot_general(
                picked.astype(BF16), tile_row(b), (((1,), (1,)), ((), ())), preferred_element_type=F32,
            ))

        square = functools.reduce(jnp.add, chunks(residual * residual))
        sums = [
            jnp.sum(square, axis=0, keepdims=True),
            total([drag * square] + [c * c for c in coupled]),
        ]
        if it:
            mixed = functools.reduce(jnp.add, chunks(residual * direction))
            sums.append(total([drag * mixed] + [c * t for c, t in zip(coupled, track)]))
        else:
            sums.append(jnp.zeros((1, 128), F32))
        part_ax[it, me_a] = jnp.concatenate(sums, axis=1)
        for step in range(1, n_ax):
            ax_copy(it, step).start()

        for b in range(blocks):
            back = jnp.dot(coupled[b].astype(BF16), tile_row(b), preferred_element_type=F32)
            for k in range(count):
                spread[b * count + k] = back[:, k * width:(k + 1) * width]
        listed_spread = jnp.concatenate([spread[:, c, :] for c in range(3)], axis=1)
        high = listed_spread.astype(BF16)
        low = (listed_spread - high.astype(F32)).astype(BF16)
        ret_out[it] = jnp.dot(
            selector, jnp.concatenate([high, low], axis=0), preferred_element_type=F32
        )
        for d in range(4):
            guarded(d, lambda d=d: ret_copy(it, d).start())

        wait_for(part_ax.at[it, pl.ds(0, n_ax - 1)], ax_recv.at[it])
        part_cr[it, me_c] = functools.reduce(jnp.add, [part_ax[it, i] for i in range(n_ax)])
        for step in range(1, n_cr):
            cr_copy(it, step).start()

        if last:
            gathered = [0.0] * 9
            for d in (1, 2):
                guarded(d, lambda d=d: wait_for(rows_in.at[d], rows_recv.at[d]))
                rows = rows_in[d]
                fields = [near_velocity[d], near[d], near_direction[d]]
                stack = jnp.concatenate([part for f in fields for part in chunks(f)], axis=0)
                first = stack.astype(BF16)
                rest = stack - first.astype(F32)
                second = rest.astype(BF16)
                third = (rest - second.astype(F32)).astype(BF16)
                bead = lax.broadcasted_iota(jnp.int32, (width, 128), 0)
                onehot = jnp.where(bead == (rows & (width - 1)), 1.0, 0.0).astype(BF16)
                found = sum(
                    jnp.dot(piece, onehot, preferred_element_type=F32) for piece in (third, second, first)
                )
                block = lax.broadcasted_iota(jnp.int32, (blocks, 128), 0)
                mine = block == (rows >> (width.bit_length() - 1))
                for n in range(9):
                    part = jnp.where(mine, found[n * blocks:(n + 1) * blocks], 0.0)
                    gathered[n] = gathered[n] + jnp.sum(part, axis=0, keepdims=True)

        arrived_all(ret_in.at[it], ret_recv.at[it])
        product = drag3 * residual + ret_out[it, CENTRE * blocks:(CENTRE + 1) * blocks]
        for d in range(4):
            product = product + ret_in[it, d]
        if not last:
            own[it + 1] = product
            for d in range(4):
                guarded(d, lambda d=d: halo_copy(it + 1, d).start())

        wait_for(part_cr.at[it, pl.ds(0, n_cr - 1)], cr_recv.at[it])
        summed = functools.reduce(jnp.add, [part_cr[it, i] for i in range(n_cr)])
        norm, energy, cross = [jnp.sum(s, axis=1, keepdims=True) for s in chunks(summed)]
        if it:
            beta = norm / norm_before
            energy = energy + 2.0 * beta * cross + beta * beta * energy_before
        alpha = norm / energy
        norm_before, energy_before = norm, energy

        def follow(now, before):
            return now + beta * before if it else now

        image = follow(product, image)
        direction = follow(residual, direction)
        velocity = velocity + alpha * direction if it else alpha * direction
        residual = residual - alpha * image
        if last:
            break
        track = [follow(c, t) for c, t in zip(coupled, track)]
        arrived_all(halo.at[it + 1], halo_recv.at[it + 1])
        for d in range(4):
            near_image[d] = follow(halo[it + 1, d], near_image[d])
            if d in (1, 2):
                near_direction[d] = follow(near[d], near_direction[d])
                step_v = alpha * near_direction[d]
                near_velocity[d] = near_velocity[d] + step_v if it else step_v
            near[d] = near[d] - alpha * near_image[d]

    for c in range(3):
        vel_ref[c] = chunks(velocity)[c]
        res_ref[c] = chunks(residual)[c]
    for c in range(3):
        row = gathered[c] + alpha * (gathered[3 + c] + beta * gathered[6 + c])
        arr_ref[c] = pltpu.roll(row, 64, 1)

    for d in (1, 2):
        guarded(d, lambda d=d: wait_for(rows_out.at[d], rows_send.at[d]))
    for d in range(4):
        guarded(d, lambda d=d: wait_for(own, halo_send.at[d]))
        guarded(d, lambda d=d: wait_for(own, ret_send.at[d]))
    wait_for(part_ax.at[:, pl.ds(0, n_ax - 1)], ax_send)
    wait_for(part_cr.at[:, pl.ds(0, n_cr - 1)], cr_send)


def write_out(vel_in, res_in, arr_in, vel_ref, res_ref, arr_ref, sem):
    moves = ((vel_in, vel_ref), (res_in, res_ref), (arr_in, arr_ref))
    copies = [pltpu.make_async_copy(a, b, sem.at[n]) for n, (a, b) in enumerate(moves)]
    for copy in copies:
        copy.start()
    for copy in copies:
        copy.wait()


def on_device(n_ax, n_cr, force, self_drag, tiles, tile_ids, mig_rows, mig_count):
    blocks, width = force.shape[2], force.shape[4]
    count = tiles.shape[3]
    field = (blocks, 3 * width)
    vmem = pl.BlockSpec(memory_space=pltpu.VMEM)
    dma = pltpu.SemaphoreType.DMA
    hbm = pl.BlockSpec(memory_space=pltpu.HBM)
    solved = pl.pallas_call(
        functools.partial(kernel, n_ax, n_cr),
        out_shape=(
            jax.ShapeDtypeStruct((3, blocks, width), F32),
            jax.ShapeDtypeStruct((3, blocks, width), F32),
            jax.ShapeDtypeStruct((3, 1, 2 * mig_rows.shape[3]), F32),
        ),
        in_specs=[hbm] * 6,
        out_specs=(vmem, vmem, vmem),
        scratch_shapes=[
            pltpu.SMEM((blocks, count), jnp.int32),
            pltpu.SMEM((2,), jnp.int32),
            pltpu.VMEM((3, blocks, width), F32),
            pltpu.VMEM((blocks, width), F32),
            pltpu.VMEM(mig_rows.shape[2:], jnp.int32),
            pltpu.VMEM((blocks, count, width, width), BF16),
            pltpu.VMEM((8 * blocks, 8, width), F32),
            pltpu.VMEM((blocks * count, 8, width), F32),
            pltpu.VMEM((ITERS,) + field, F32),
            pltpu.VMEM((ITERS, 4) + field, F32),
            pltpu.VMEM((ITERS, 8 * blocks, 3 * width), F32),
            pltpu.VMEM((ITERS, 4) + field, F32),
            pltpu.VMEM((ITERS, n_ax, 1, 384), F32),
            pltpu.VMEM((ITERS, n_cr, 1, 384), F32),
            pltpu.VMEM((8, 128), jnp.int32),
            pltpu.VMEM((3, 1, 128), jnp.int32),
            pltpu.VMEM((3, 1, 128), jnp.int32),
            dma, dma((5,)),
            dma((4,)), dma((ITERS,)),
            dma((4,)), dma((ITERS,)),
            dma((3,)), dma((3,)),
            dma, dma((ITERS,)),
            dma, dma((ITERS,)),
        ],
        compiler_params=pltpu.CompilerParams(
            collective_id=0, has_side_effects=True, vmem_limit_bytes=60 * 1024 * 1024
        ),
        name="cg_solve",
    )(
        tile_ids.reshape(tile_ids.shape[2:]),
        mig_count.reshape(mig_count.shape[2:]),
        jnp.swapaxes(force[0, 0], 0, 1),
        self_drag.reshape(self_drag.shape[2:]),
        tiles.reshape(tiles.shape[2:]),
        mig_rows.reshape(mig_rows.shape[2:]),
    )
    velocity, residual, arrivals = pl.pallas_call(
        write_out,
        out_shape=tuple(jax.ShapeDtypeStruct(x.shape, x.dtype) for x in solved),
        in_specs=[hbm] * 3,
        out_specs=(hbm,) * 3,
        scratch_shapes=[dma((3,))],
        name="write_out",
    )(*solved)
    velocity, residual = jnp.swapaxes(velocity, 0, 1), jnp.swapaxes(residual, 0, 1)
    return velocity[None, None], residual[None, None], arrivals[:, 0][None, None]


def solution(mesh):
    placed = (
        P("axial", "cross", None, None, None),
        P("axial", "cross", None, None),
        P("axial", "cross", None, None, None, None),
        P("axial", "cross", None, None),
        P("axial", "cross", None, None),
        P("axial", "cross", None),
    )
    return jax.shard_map(
        functools.partial(on_device, mesh.shape["axial"], mesh.shape["cross"]),
        mesh=mesh,
        in_specs=placed,
        out_specs=(
            P("axial", "cross", None, None, None),
            P("axial", "cross", None, None, None),
            P("axial", "cross", None, None),
        ),
        check_vma=False,
    )
```

```python
import functools

import jax
import jax.numpy as jnp
from jax import lax
from jax.experimental import pallas as pl
from jax.experimental.pallas import tpu as pltpu
from jax.sharding import PartitionSpec as P

ITERS = 3
MESH = pl.DeviceIdType.MESH
PLACES = (1, 3, 5, 7)
CENTRE = 4
F32 = jnp.float32
BF16 = jnp.bfloat16


def chunks(field):
    return [field[:, c * 128:(c + 1) * 128] for c in range(3)]


def kernel(
    n_ax, n_cr,
    ids_hbm, count_hbm, force_hbm, drag_hbm, tiles_ref, rows_hbm,
    vel_ref, res_ref, arr_ref,
    ids_ref, count_ref, force_ref, drag_ref, rows_ref, tile_buf, tile_turned, ext, spread, own, halo, ret_out, ret_in, part_ax, part_cr, mig, rows_out, rows_in,
    tile_sem, small_sem, halo_send, halo_recv, ret_send, ret_recv, rows_send, rows_recv,
    ax_send, ax_recv, cr_send, cr_recv,
):
    blocks, count, width = tiles_ref.shape[0], tiles_ref.shape[1], tiles_ref.shape[2]
    pairs = blocks * count
    slot = rows_hbm.shape[1]
    me_a = lax.axis_index("axial")
    me_c = lax.axis_index("cross")

    def ax_peer(step):
        return {"axial": lax.rem(me_a + step, n_ax)}

    def cr_peer(step):
        return {"cross": lax.rem(me_c + step, n_cr)}

    device = (ax_peer(n_ax - 1), cr_peer(n_cr - 1), cr_peer(1), ax_peer(1))
    exists = (None, me_c > 0, me_c + 1 < n_cr, None)

    def guarded(d, act):
        if exists[d] is None:
            act()
        else:
            pl.when(exists[d])(act)

    def neighbour(src, dst, send, recv, d):
        return pltpu.make_async_remote_copy(
            src_ref=src, dst_ref=dst.at[3 - d], send_sem=send, recv_sem=recv,
            device_id=device[d], device_id_type=MESH,
        )

    def halo_copy(stage, d):
        return neighbour(own.at[stage], halo.at[stage], halo_send.at[d], halo_recv.at[stage], d)

    def ret_copy(it, d):
        src = ret_out.at[it, pl.ds(PLACES[d] * blocks, blocks)]
        return neighbour(src, ret_in.at[it], ret_send.at[d], ret_recv.at[it], d)

    def rows_copy(d):
        return neighbour(rows_out.at[d], rows_in, rows_send.at[d], rows_recv.at[3 - d], d)

    def wait_for(ref, sem):
        pltpu.make_async_copy(ref, ref, sem).wait()

    inner = exists[1] & exists[2]

    def arrived_all(ref, sem):
        @pl.when(inner)
        def _():
            wait_for(ref, sem)

        @pl.when(jnp.logical_not(inner))
        def _():
            wait_for(ref.at[pl.ds(0, 3)], sem)

    def ax_copy(it, step):
        return pltpu.make_async_remote_copy(
            src_ref=part_ax.at[it, me_a], dst_ref=part_ax.at[it, me_a],
            send_sem=ax_send, recv_sem=ax_recv.at[it],
            device_id=ax_peer(step), device_id_type=MESH,
        )

    def cr_copy(it, step):
        return pltpu.make_async_remote_copy(
            src_ref=part_cr.at[it, me_c], dst_ref=part_cr.at[it, me_c],
            send_sem=cr_send, recv_sem=cr_recv.at[it],
            device_id=cr_peer(step), device_id_type=MESH,
        )

    fetched = (
        (force_hbm, force_ref), (ids_hbm, ids_ref), (count_hbm, count_ref),
        (drag_hbm, drag_ref), (rows_hbm, rows_ref),
    )
    small = [pltpu.make_async_copy(a, b, small_sem.at[n]) for n, (a, b) in enumerate(fetched)]
    for copy in small:
        copy.start()

    barrier = pltpu.get_barrier_semaphore()
    for step in range(1, n_ax):
        pl.semaphore_signal(barrier, inc=1, device_id=ax_peer(step), device_id_type=MESH)
    for step in range(1, n_cr):
        pl.semaphore_signal(barrier, inc=1, device_id=cr_peer(step), device_id_type=MESH)

    load = pltpu.make_async_copy(tiles_ref, tile_buf, tile_sem)
    load.start()
    for copy in small:
        copy.wait()

    force = jnp.concatenate([force_ref[c] for c in range(3)], axis=1)
    own[0] = force
    lane = lax.broadcasted_iota(jnp.int32, (1, 128), 1)
    mig[0:2, 0:slot] = rows_ref[...]
    listed = mig[...]
    turned = pltpu.roll(listed, 64, 1)
    rows_out[1] = jnp.where((lane < slot) & (lane < count_ref[0]), listed[0:1], -1)
    rows_out[2] = jnp.where((lane >= 64) & (lane - 64 < count_ref[1]), turned[1:2], -1)

    for d in (1, 2):
        @pl.when(jnp.logical_not(exists[d]))
        def _():
            for stage in range(ITERS):
                halo[stage, d] = jnp.zeros((blocks, 3 * width), F32)
                ret_in[stage, d] = jnp.zeros((blocks, 3 * width), F32)
            rows_in[d] = jnp.full((1, 128), -1, jnp.int32)

    pl.semaphore_wait(barrier, n_ax - 1 + n_cr - 1)

    for d in range(4):
        guarded(d, lambda d=d: halo_copy(0, d).start())
    for d in (1, 2):
        guarded(d, lambda d=d: rows_copy(d).start())

    ext[...] = jnp.zeros(ext.shape, F32)
    wide = lax.broadcasted_iota(jnp.int32, (1, 2 * pairs), 1)
    listed_ids = jnp.zeros((1, 2 * pairs), jnp.int32)
    for n in range(pairs):
        hit = (wide == n) | (wide == n + pairs)
        listed_ids = jnp.where(hit, ids_ref[n // count, n % count], listed_ids)
    entry = lax.broadcasted_iota(jnp.int32, (8 * blocks, 2 * pairs), 0)
    selector = jnp.where(entry == listed_ids, 1.0, 0.0).astype(BF16)
    drag = drag_ref[...]
    drag3 = jnp.concatenate([drag] * 3, axis=1)

    def place(p, field):
        for c, part in enumerate(chunks(field)):
            ext[p * blocks:(p + 1) * blocks, c, :] = part

    def tile_row(b):
        return jnp.concatenate([tile_buf[b, k] for k in range(count)], axis=1)

    def total(parts):
        return jnp.sum(functools.reduce(jnp.add, parts), axis=0, keepdims=True)

    place(CENTRE, force)
    residual = force
    velocity = direction = image = None
    near = [None] * 4
    near_image = [None] * 4
    near_velocity = [None] * 4
    near_direction = [None] * 4
    track = [None] * blocks
    norm_before = energy_before = None

    load.wait()
    for b in range(blocks):
        for k in range(count):
            tile_turned[b, k * width:(k + 1) * width] = tile_buf[b, k].T
    arrived_all(halo.at[0], halo_recv.at[0])
    for d in range(4):
        near[d] = halo[0, d]

    for it in range(ITERS):
        last = it == ITERS - 1
        if it:
            place(CENTRE, residual)
        for d in range(4):
            place(PLACES[d], near[d])
        coupled = []
        for b in range(blocks):
            picked = jnp.concatenate([ext[ids_ref[b, k]] for k in range(count)], axis=1)
            coupled.append(jnp.dot(picked.astype(BF16), tile_turned[b], preferred_element_type=F32))

        square = functools.reduce(jnp.add, chunks(residual * residual))
        sums = [
            jnp.sum(square, axis=0, keepdims=True),
            total([drag * square] + [c * c for c in coupled]),
        ]
        if it:
            mixed = functools.reduce(jnp.add, chunks(residual * direction))
            sums.append(total([drag * mixed] + [c * t for c, t in zip(coupled, track)]))
        else:
            sums.append(jnp.zeros((1, 128), F32))
        part_ax[it, me_a] = jnp.concatenate(sums, axis=1)
        for step in range(1, n_ax):
            ax_copy(it, step).start()

        for b in range(blocks):
            back = jnp.dot(coupled[b].astype(BF16), tile_row(b), preferred_element_type=F32)
            for k in range(count):
                spread[b * count + k] = back[:, k * width:(k + 1) * width]
        listed_spread = jnp.concatenate([spread[:, c, :] for c in range(3)], axis=1)
        high = listed_spread.astype(BF16)
        low = (listed_spread - high.astype(F32)).astype(BF16)
        ret_out[it] = jnp.dot(
            selector, jnp.concatenate([high, low], axis=0), preferred_element_type=F32
        )
        for d in range(4):
            guarded(d, lambda d=d: ret_copy(it, d).start())

        wait_for(part_ax.at[it, pl.ds(0, n_ax - 1)], ax_recv.at[it])
        part_cr[it, me_c] = functools.reduce(jnp.add, [part_ax[it, i] for i in range(n_ax)])
        for step in range(1, n_cr):
            cr_copy(it, step).start()

        if last:
            gathered = [0.0] * 9
            for d in (1, 2):
                guarded(d, lambda d=d: wait_for(rows_in.at[d], rows_recv.at[d]))
                rows = rows_in[d]
                fields = [near_velocity[d], near[d], near_direction[d]]
                stack = jnp.concatenate([part for f in fields for part in chunks(f)], axis=0)
                first = stack.astype(BF16)
                rest = stack - first.astype(F32)
                second = rest.astype(BF16)
                third = (rest - second.astype(F32)).astype(BF16)
                bead = lax.broadcasted_iota(jnp.int32, (width, 128), 0)
                onehot = jnp.where(bead == (rows & (width - 1)), 1.0, 0.0).astype(BF16)
                found = sum(
                    jnp.dot(piece, onehot, preferred_element_type=F32) for piece in (third, second, first)
                )
                block = lax.broadcasted_iota(jnp.int32, (blocks, 128), 0)
                mine = block == (rows >> (width.bit_length() - 1))
                for n in range(9):
                    part = jnp.where(mine, found[n * blocks:(n + 1) * blocks], 0.0)
                    gathered[n] = gathered[n] + jnp.sum(part, axis=0, keepdims=True)

        arrived_all(ret_in.at[it], ret_recv.at[it])
        product = drag3 * residual + ret_out[it, CENTRE * blocks:(CENTRE + 1) * blocks]
        for d in range(4):
            product = product + ret_in[it, d]
        if not last:
            own[it + 1] = product
            for d in range(4):
                guarded(d, lambda d=d: halo_copy(it + 1, d).start())

        wait_for(part_cr.at[it, pl.ds(0, n_cr - 1)], cr_recv.at[it])
        summed = functools.reduce(jnp.add, [part_cr[it, i] for i in range(n_cr)])
        norm, energy, cross = [jnp.sum(s, axis=1, keepdims=True) for s in chunks(summed)]
        if it:
            beta = norm / norm_before
            energy = energy + 2.0 * beta * cross + beta * beta * energy_before
        alpha = norm / energy
        norm_before, energy_before = norm, energy

        def follow(now, before):
            return now + beta * before if it else now

        image = follow(product, image)
        direction = follow(residual, direction)
        velocity = velocity + alpha * direction if it else alpha * direction
        residual = residual - alpha * image
        if last:
            break
        track = [follow(c, t) for c, t in zip(coupled, track)]
        arrived_all(halo.at[it + 1], halo_recv.at[it + 1])
        for d in range(4):
            near_image[d] = follow(halo[it + 1, d], near_image[d])
            if d in (1, 2):
                near_direction[d] = follow(near[d], near_direction[d])
                step_v = alpha * near_direction[d]
                near_velocity[d] = near_velocity[d] + step_v if it else step_v
            near[d] = near[d] - alpha * near_image[d]

    for c in range(3):
        vel_ref[c] = chunks(velocity)[c]
        res_ref[c] = chunks(residual)[c]
    for c in range(3):
        row = gathered[c] + alpha * (gathered[3 + c] + beta * gathered[6 + c])
        arr_ref[c] = pltpu.roll(row, 64, 1)

    for d in (1, 2):
        guarded(d, lambda d=d: wait_for(rows_out.at[d], rows_send.at[d]))
    for d in range(4):
        guarded(d, lambda d=d: wait_for(own, halo_send.at[d]))
        guarded(d, lambda d=d: wait_for(own, ret_send.at[d]))
    wait_for(part_ax.at[:, pl.ds(0, n_ax - 1)], ax_send)
    wait_for(part_cr.at[:, pl.ds(0, n_cr - 1)], cr_send)


def write_out(vel_in, res_in, arr_in, vel_ref, res_ref, arr_ref, sem):
    moves = ((vel_in, vel_ref), (res_in, res_ref), (arr_in, arr_ref))
    copies = [pltpu.make_async_copy(a, b, sem.at[n]) for n, (a, b) in enumerate(moves)]
    for copy in copies:
        copy.start()
    for copy in copies:
        copy.wait()


def on_device(n_ax, n_cr, force, self_drag, tiles, tile_ids, mig_rows, mig_count):
    blocks, width = force.shape[2], force.shape[4]
    count = tiles.shape[3]
    field = (blocks, 3 * width)
    vmem = pl.BlockSpec(memory_space=pltpu.VMEM)
    dma = pltpu.SemaphoreType.DMA
    hbm = pl.BlockSpec(memory_space=pltpu.HBM)
    solved = pl.pallas_call(
        functools.partial(kernel, n_ax, n_cr),
        out_shape=(
            pltpu.VMEM((3, blocks, width), F32),
            pltpu.VMEM((3, blocks, width), F32),
            pltpu.VMEM((3, 1, 2 * mig_rows.shape[3]), F32),
        ),
        in_specs=[hbm] * 6,
        out_specs=(vmem, vmem, vmem),
        scratch_shapes=[
            pltpu.SMEM((blocks, count), jnp.int32),
            pltpu.SMEM((2,), jnp.int32),
            pltpu.VMEM((3, blocks, width), F32),
            pltpu.VMEM((blocks, width), F32),
            pltpu.VMEM(mig_rows.shape[2:], jnp.int32),
            pltpu.VMEM((blocks, count, width, width), BF16),
            pltpu.VMEM((blocks, count * width, width), BF16),
            pltpu.VMEM((8 * blocks, 8, width), F32),
            pltpu.VMEM((blocks * count, 8, width), F32),
            pltpu.VMEM((ITERS,) + field, F32),
            pltpu.VMEM((ITERS, 4) + field, F32),
            pltpu.VMEM((ITERS, 8 * blocks, 3 * width), F32),
            pltpu.VMEM((ITERS, 4) + field, F32),
            pltpu.VMEM((ITERS, n_ax, 1, 384), F32),
            pltpu.VMEM((ITERS, n_cr, 1, 384), F32),
            pltpu.VMEM((8, 128), jnp.int32),
            pltpu.VMEM((3, 1, 128), jnp.int32),
            pltpu.VMEM((3, 1, 128), jnp.int32),
            dma, dma((5,)),
            dma((4,)), dma((ITERS,)),
            dma((4,)), dma((ITERS,)),
            dma((3,)), dma((3,)),
            dma, dma((ITERS,)),
            dma, dma((ITERS,)),
        ],
        compiler_params=pltpu.CompilerParams(
            collective_id=0, has_side_effects=True, vmem_limit_bytes=60 * 1024 * 1024
        ),
        name="cg_solve",
    )(
        tile_ids.reshape(tile_ids.shape[2:]),
        mig_count.reshape(mig_count.shape[2:]),
        jnp.swapaxes(force[0, 0], 0, 1),
        self_drag.reshape(self_drag.shape[2:]),
        tiles.reshape(tiles.shape[2:]),
        mig_rows.reshape(mig_rows.shape[2:]),
    )
    velocity, residual, arrivals = pl.pallas_call(
        write_out,
        out_shape=tuple(jax.ShapeDtypeStruct(x.shape, x.dtype) for x in solved),
        in_specs=[vmem] * 3,
        out_specs=(hbm,) * 3,
        scratch_shapes=[dma((3,))],
        name="write_out",
    )(*solved)
    velocity, residual = jnp.swapaxes(velocity, 0, 1), jnp.swapaxes(residual, 0, 1)
    return velocity[None, None], residual[None, None], arrivals[:, 0][None, None]


def solution(mesh):
    placed = (
        P("axial", "cross", None, None, None),
        P("axial", "cross", None, None),
        P("axial", "cross", None, None, None, None),
        P("axial", "cross", None, None),
        P("axial", "cross", None, None),
        P("axial", "cross", None),
    )
    return jax.shard_map(
        functools.partial(on_device, mesh.shape["axial"], mesh.shape["cross"]),
        mesh=mesh,
        in_specs=placed,
        out_specs=(
            P("axial", "cross", None, None, None),
            P("axial", "cross", None, None, None),
            P("axial", "cross", None, None),
        ),
        check_vma=False,
    )
```

```python
import functools

import jax
import jax.numpy as jnp
from jax import lax
from jax.experimental import pallas as pl
from jax.experimental.pallas import tpu as pltpu
from jax.sharding import PartitionSpec as P

ITERS = 3
MESH = pl.DeviceIdType.MESH
PLACES = (1, 3, 5, 7)
CENTRE = 4
F32 = jnp.float32
BF16 = jnp.bfloat16


def chunks(field):
    return [field[:, c * 128:(c + 1) * 128] for c in range(3)]


def kernel(
    n_ax, n_cr,
    ids_hbm, count_hbm, force_hbm, drag_hbm, tiles_ref, rows_hbm,
    vel_ref, res_ref, arr_ref,
    ids_ref, count_ref, force_ref, drag_ref, rows_ref, tile_buf, tile_turned, ext, spread, own, halo, ret_out, ret_in, part_ax, part_cr, mig, rows_out, rows_in,
    tile_sem, small_sem, halo_send, halo_recv, ret_send, ret_recv, rows_send, rows_recv,
    ax_send, ax_recv, cr_send, cr_recv,
):
    blocks, count, width = tiles_ref.shape[0], tiles_ref.shape[1], tiles_ref.shape[2]
    pairs = blocks * count
    slot = rows_hbm.shape[1]
    me_a = lax.axis_index("axial")
    me_c = lax.axis_index("cross")

    def ax_peer(step):
        return {"axial": lax.rem(me_a + step, n_ax)}

    def cr_peer(step):
        return {"cross": lax.rem(me_c + step, n_cr)}

    device = (ax_peer(n_ax - 1), cr_peer(n_cr - 1), cr_peer(1), ax_peer(1))
    exists = (None, me_c > 0, me_c + 1 < n_cr, None)

    def guarded(d, act):
        if exists[d] is None:
            act()
        else:
            pl.when(exists[d])(act)

    def neighbour(src, dst, send, recv, d):
        return pltpu.make_async_remote_copy(
            src_ref=src, dst_ref=dst.at[3 - d], send_sem=send, recv_sem=recv,
            device_id=device[d], device_id_type=MESH,
        )

    def halo_copy(stage, d):
        return neighbour(own.at[stage], halo.at[stage], halo_send.at[d], halo_recv.at[stage], d)

    def ret_copy(it, d):
        src = ret_out.at[it, pl.ds(PLACES[d] * blocks, blocks)]
        return neighbour(src, ret_in.at[it], ret_send.at[d], ret_recv.at[it], d)

    def rows_copy(d):
        return neighbour(rows_out.at[d], rows_in, rows_send.at[d], rows_recv.at[3 - d], d)

    def wait_for(ref, sem):
        pltpu.make_async_copy(ref, ref, sem).wait()

    inner = exists[1] & exists[2]

    def arrived_all(ref, sem):
        @pl.when(inner)
        def _():
            wait_for(ref, sem)

        @pl.when(jnp.logical_not(inner))
        def _():
            wait_for(ref.at[pl.ds(0, 3)], sem)

    def ax_copy(it, step):
        return pltpu.make_async_remote_copy(
            src_ref=part_ax.at[it, me_a], dst_ref=part_ax.at[it, me_a],
            send_sem=ax_send, recv_sem=ax_recv.at[it],
            device_id=ax_peer(step), device_id_type=MESH,
        )

    def cr_copy(it, step):
        return pltpu.make_async_remote_copy(
            src_ref=part_cr.at[it, me_c], dst_ref=part_cr.at[it, me_c],
            send_sem=cr_send, recv_sem=cr_recv.at[it],
            device_id=cr_peer(step), device_id_type=MESH,
        )

    fetched = (
        (force_hbm, force_ref), (ids_hbm, ids_ref), (count_hbm, count_ref),
        (drag_hbm, drag_ref), (rows_hbm, rows_ref),
    )
    small = [pltpu.make_async_copy(a, b, small_sem.at[n]) for n, (a, b) in enumerate(fetched)]
    for copy in small:
        copy.start()

    barrier = pltpu.get_barrier_semaphore()
    for step in range(1, n_ax):
        pl.semaphore_signal(barrier, inc=1, device_id=ax_peer(step), device_id_type=MESH)
    for step in range(1, n_cr):
        pl.semaphore_signal(barrier, inc=1, device_id=cr_peer(step), device_id_type=MESH)

    load = pltpu.make_async_copy(tiles_ref, tile_buf, tile_sem)
    load.start()
    for copy in small:
        copy.wait()

    force = jnp.concatenate([force_ref[c] for c in range(3)], axis=1)
    own[0] = force
    lane = lax.broadcasted_iota(jnp.int32, (1, 128), 1)
    mig[0:2, 0:slot] = rows_ref[...]
    listed = mig[...]
    turned = pltpu.roll(listed, 64, 1)
    rows_out[1] = jnp.where((lane < slot) & (lane < count_ref[0]), listed[0:1], -1)
    rows_out[2] = jnp.where((lane >= 64) & (lane - 64 < count_ref[1]), turned[1:2], -1)

    for d in (1, 2):
        @pl.when(jnp.logical_not(exists[d]))
        def _():
            for stage in range(ITERS):
                halo[stage, d] = jnp.zeros((blocks, 3 * width), F32)
                ret_in[stage, d] = jnp.zeros((blocks, 3 * width), F32)
            rows_in[d] = jnp.full((1, 128), -1, jnp.int32)

    pl.semaphore_wait(barrier, n_ax - 1 + n_cr - 1)

    for d in range(4):
        guarded(d, lambda d=d: halo_copy(0, d).start())
    for d in (1, 2):
        guarded(d, lambda d=d: rows_copy(d).start())

    ext[...] = jnp.zeros(ext.shape, F32)
    wide = lax.broadcasted_iota(jnp.int32, (1, 2 * pairs), 1)
    listed_ids = jnp.zeros((1, 2 * pairs), jnp.int32)
    for n in range(pairs):
        hit = (wide == n) | (wide == n + pairs)
        listed_ids = jnp.where(hit, ids_ref[n // count, n % count], listed_ids)
    entry = lax.broadcasted_iota(jnp.int32, (8 * blocks, 2 * pairs), 0)
    selector = jnp.where(entry == listed_ids, 1.0, 0.0).astype(BF16)
    drag = drag_ref[...]
    drag3 = jnp.concatenate([drag] * 3, axis=1)

    def place(p, field):
        for c, part in enumerate(chunks(field)):
            ext[p * blocks:(p + 1) * blocks, c, :] = part

    def tile_row(b):
        return jnp.concatenate([tile_buf[b, k] for k in range(count)], axis=1)

    def total(parts):
        return jnp.sum(functools.reduce(jnp.add, parts), axis=0, keepdims=True)

    place(CENTRE, force)
    residual = force
    velocity = direction = image = None
    near = [None] * 4
    near_image = [None] * 4
    near_velocity = [None] * 4
    near_direction = [None] * 4
    track = [None] * blocks
    norm_before = energy_before = None

    load.wait()
    for b in range(blocks):
        for k in range(count):
            side = (b % 2) * width
            tile_turned[b // 2, k * width:(k + 1) * width, side:side + width] = tile_buf[b, k].T
    arrived_all(halo.at[0], halo_recv.at[0])
    for d in range(4):
        near[d] = halo[0, d]

    for it in range(ITERS):
        last = it == ITERS - 1
        if it:
            place(CENTRE, residual)
        for d in range(4):
            place(PLACES[d], near[d])
        coupled = []
        for b in range(0, blocks, 2):
            picked = jnp.concatenate([
                jnp.concatenate([ext[ids_ref[b + s, k]] for k in range(count)], axis=1) for s in range(2)
            ], axis=0)
            pair = jnp.dot(picked.astype(BF16), tile_turned[b // 2], preferred_element_type=F32)
            coupled += [pair[0:8, 0:width], pair[8:16, width:2 * width]]

        square = functools.reduce(jnp.add, chunks(residual * residual))
        sums = [
            jnp.sum(square, axis=0, keepdims=True),
            total([drag * square] + [c * c for c in coupled]),
        ]
        if it:
            mixed = functools.reduce(jnp.add, chunks(residual * direction))
            sums.append(total([drag * mixed] + [c * t for c, t in zip(coupled, track)]))
        else:
            sums.append(jnp.zeros((1, 128), F32))
        part_ax[it, me_a] = jnp.concatenate(sums, axis=1)
        for step in range(1, n_ax):
            ax_copy(it, step).start()

        for b in range(0, blocks, 2):
            blank = jnp.zeros((8, width), F32)
            diagonal = jnp.concatenate([
                jnp.concatenate([coupled[b], blank], axis=1),
                jnp.concatenate([blank, coupled[b + 1]], axis=1),
            ], axis=0)
            both = jnp.concatenate([tile_row(b), tile_row(b + 1)], axis=0)
            back = jnp.dot(diagonal.astype(BF16), both, preferred_element_type=F32)
            for k in range(count):
                spread[b * count + k] = back[0:8, k * width:(k + 1) * width]
                spread[(b + 1) * count + k] = back[8:16, k * width:(k + 1) * width]
        listed_spread = jnp.concatenate([spread[:, c, :] for c in range(3)], axis=1)
        high = listed_spread.astype(BF16)
        low = (listed_spread - high.astype(F32)).astype(BF16)
        ret_out[it] = jnp.dot(
            selector, jnp.concatenate([high, low], axis=0), preferred_element_type=F32
        )
        for d in range(4):
            guarded(d, lambda d=d: ret_copy(it, d).start())

        wait_for(part_ax.at[it, pl.ds(0, n_ax - 1)], ax_recv.at[it])
        part_cr[it, me_c] = functools.reduce(jnp.add, [part_ax[it, i] for i in range(n_ax)])
        for step in range(1, n_cr):
            cr_copy(it, step).start()

        if last:
            gathered = [0.0] * 9
            for d in (1, 2):
                guarded(d, lambda d=d: wait_for(rows_in.at[d], rows_recv.at[d]))
                rows = rows_in[d]
                fields = [near_velocity[d], near[d], near_direction[d]]
                stack = jnp.concatenate([part for f in fields for part in chunks(f)], axis=0)
                first = stack.astype(BF16)
                rest = stack - first.astype(F32)
                second = rest.astype(BF16)
                third = (rest - second.astype(F32)).astype(BF16)
                bead = lax.broadcasted_iota(jnp.int32, (width, 128), 0)
                onehot = jnp.where(bead == (rows & (width - 1)), 1.0, 0.0).astype(BF16)
                found = sum(
                    jnp.dot(piece, onehot, preferred_element_type=F32) for piece in (third, second, first)
                )
                block = lax.broadcasted_iota(jnp.int32, (blocks, 128), 0)
                mine = block == (rows >> (width.bit_length() - 1))
                for n in range(9):
                    part = jnp.where(mine, found[n * blocks:(n + 1) * blocks], 0.0)
                    gathered[n] = gathered[n] + jnp.sum(part, axis=0, keepdims=True)

        arrived_all(ret_in.at[it], ret_recv.at[it])
        product = drag3 * residual + ret_out[it, CENTRE * blocks:(CENTRE + 1) * blocks]
        for d in range(4):
            product = product + ret_in[it, d]
        if not last:
            own[it + 1] = product
            for d in range(4):
                guarded(d, lambda d=d: halo_copy(it + 1, d).start())

        wait_for(part_cr.at[it, pl.ds(0, n_cr - 1)], cr_recv.at[it])
        summed = functools.reduce(jnp.add, [part_cr[it, i] for i in range(n_cr)])
        norm, energy, cross = [jnp.sum(s, axis=1, keepdims=True) for s in chunks(summed)]
        if it:
            beta = norm / norm_before
            energy = energy + 2.0 * beta * cross + beta * beta * energy_before
        alpha = norm / energy
        norm_before, energy_before = norm, energy

        def follow(now, before):
            return now + beta * before if it else now

        image = follow(product, image)
        direction = follow(residual, direction)
        velocity = velocity + alpha * direction if it else alpha * direction
        residual = residual - alpha * image
        if last:
            break
        track = [follow(c, t) for c, t in zip(coupled, track)]
        arrived_all(halo.at[it + 1], halo_recv.at[it + 1])
        for d in range(4):
            near_image[d] = follow(halo[it + 1, d], near_image[d])
            if d in (1, 2):
                near_direction[d] = follow(near[d], near_direction[d])
                step_v = alpha * near_direction[d]
                near_velocity[d] = near_velocity[d] + step_v if it else step_v
            near[d] = near[d] - alpha * near_image[d]

    for c in range(3):
        vel_ref[c] = chunks(velocity)[c]
        res_ref[c] = chunks(residual)[c]
    for c in range(3):
        row = gathered[c] + alpha * (gathered[3 + c] + beta * gathered[6 + c])
        arr_ref[c] = pltpu.roll(row, 64, 1)

    for d in (1, 2):
        guarded(d, lambda d=d: wait_for(rows_out.at[d], rows_send.at[d]))
    for d in range(4):
        guarded(d, lambda d=d: wait_for(own, halo_send.at[d]))
        guarded(d, lambda d=d: wait_for(own, ret_send.at[d]))
    wait_for(part_ax.at[:, pl.ds(0, n_ax - 1)], ax_send)
    wait_for(part_cr.at[:, pl.ds(0, n_cr - 1)], cr_send)


def write_out(vel_in, res_in, arr_in, vel_ref, res_ref, arr_ref, sem):
    moves = ((vel_in, vel_ref), (res_in, res_ref), (arr_in, arr_ref))
    copies = [pltpu.make_async_copy(a, b, sem.at[n]) for n, (a, b) in enumerate(moves)]
    for copy in copies:
        copy.start()
    for copy in copies:
        copy.wait()


def on_device(n_ax, n_cr, force, self_drag, tiles, tile_ids, mig_rows, mig_count):
    blocks, width = force.shape[2], force.shape[4]
    count = tiles.shape[3]
    field = (blocks, 3 * width)
    vmem = pl.BlockSpec(memory_space=pltpu.VMEM)
    dma = pltpu.SemaphoreType.DMA
    hbm = pl.BlockSpec(memory_space=pltpu.HBM)
    solved = pl.pallas_call(
        functools.partial(kernel, n_ax, n_cr),
        out_shape=(
            pltpu.VMEM((3, blocks, width), F32),
            pltpu.VMEM((3, blocks, width), F32),
            pltpu.VMEM((3, 1, 2 * mig_rows.shape[3]), F32),
        ),
        in_specs=[hbm] * 6,
        out_specs=(vmem, vmem, vmem),
        scratch_shapes=[
            pltpu.SMEM((blocks, count), jnp.int32),
            pltpu.SMEM((2,), jnp.int32),
            pltpu.VMEM((3, blocks, width), F32),
            pltpu.VMEM((blocks, width), F32),
            pltpu.VMEM(mig_rows.shape[2:], jnp.int32),
            pltpu.VMEM((blocks, count, width, width), BF16),
            pltpu.VMEM((blocks // 2, count * width, 2 * width), BF16),
            pltpu.VMEM((8 * blocks, 8, width), F32),
            pltpu.VMEM((blocks * count, 8, width), F32),
            pltpu.VMEM((ITERS,) + field, F32),
            pltpu.VMEM((ITERS, 4) + field, F32),
            pltpu.VMEM((ITERS, 8 * blocks, 3 * width), F32),
            pltpu.VMEM((ITERS, 4) + field, F32),
            pltpu.VMEM((ITERS, n_ax, 1, 384), F32),
            pltpu.VMEM((ITERS, n_cr, 1, 384), F32),
            pltpu.VMEM((8, 128), jnp.int32),
            pltpu.VMEM((3, 1, 128), jnp.int32),
            pltpu.VMEM((3, 1, 128), jnp.int32),
            dma, dma((5,)),
            dma((4,)), dma((ITERS,)),
            dma((4,)), dma((ITERS,)),
            dma((3,)), dma((3,)),
            dma, dma((ITERS,)),
            dma, dma((ITERS,)),
        ],
        compiler_params=pltpu.CompilerParams(
            collective_id=0, has_side_effects=True, vmem_limit_bytes=60 * 1024 * 1024
        ),
        name="cg_solve",
    )(
        tile_ids.reshape(tile_ids.shape[2:]),
        mig_count.reshape(mig_count.shape[2:]),
        jnp.swapaxes(force[0, 0], 0, 1),
        self_drag.reshape(self_drag.shape[2:]),
        tiles.reshape(tiles.shape[2:]),
        mig_rows.reshape(mig_rows.shape[2:]),
    )
    velocity, residual, arrivals = pl.pallas_call(
        write_out,
        out_shape=tuple(jax.ShapeDtypeStruct(x.shape, x.dtype) for x in solved),
        in_specs=[vmem] * 3,
        out_specs=(hbm,) * 3,
        scratch_shapes=[dma((3,))],
        compiler_params=pltpu.CompilerParams(vmem_limit_bytes=1024 * 1024),
        name="write_out",
    )(*solved)
    velocity, residual = jnp.swapaxes(velocity, 0, 1), jnp.swapaxes(residual, 0, 1)
    return velocity[None, None], residual[None, None], arrivals[:, 0][None, None]


def solution(mesh):
    placed = (
        P("axial", "cross", None, None, None),
        P("axial", "cross", None, None),
        P("axial", "cross", None, None, None, None),
        P("axial", "cross", None, None),
        P("axial", "cross", None, None),
        P("axial", "cross", None),
    )
    return jax.shard_map(
        functools.partial(on_device, mesh.shape["axial"], mesh.shape["cross"]),
        mesh=mesh,
        in_specs=placed,
        out_specs=(
            P("axial", "cross", None, None, None),
            P("axial", "cross", None, None, None),
            P("axial", "cross", None, None),
        ),
        check_vma=False,
    )
```

```python
import functools

import jax
import jax.numpy as jnp
from jax import lax
from jax.experimental import pallas as pl
from jax.experimental.pallas import tpu as pltpu
from jax.sharding import PartitionSpec as P

ITERS = 3
LOGICAL = pl.DeviceIdType.LOGICAL
PLACES = (1, 3, 5, 7)
CENTRE = 4
F32 = jnp.float32
BF16 = jnp.bfloat16


def chunks(field):
    return [field[:, c * 128:(c + 1) * 128] for c in range(3)]


def kernel(
    n_ax, n_cr,
    ids_hbm, count_hbm, force_hbm, drag_hbm, tiles_ref, rows_hbm,
    vel_ref, res_ref, arr_ref,
    ids_ref, count_ref, force_ref, drag_ref, rows_ref, tile_buf, tile_turned, ext, spread, own, halo, ret_out, ret_in, part_ax, part_cr, mig, rows_out, rows_in,
    tile_sem, small_sem, halo_send, halo_recv, ret_send, ret_recv, rows_send, rows_recv,
    ax_send, ax_recv, cr_send, cr_recv,
):
    blocks, count, width = tiles_ref.shape[0], tiles_ref.shape[1], tiles_ref.shape[2]
    pairs = blocks * count
    slot = rows_hbm.shape[1]
    me_a = lax.axis_index("axial")
    me_c = lax.axis_index("cross")

    me = me_a * n_cr + me_c
    ax_peers = [jnp.where(me_a + step < n_ax, me + step * n_cr, me + (step - n_ax) * n_cr) for step in range(n_ax)]
    cr_peers = [jnp.where(me_c + step < n_cr, me + step, me + (step - n_cr)) for step in range(n_cr)]

    def ax_peer(step):
        return ax_peers[step]

    def cr_peer(step):
        return cr_peers[step]

    device = (ax_peer(n_ax - 1), cr_peer(n_cr - 1), cr_peer(1), ax_peer(1))
    exists = (None, me_c > 0, me_c + 1 < n_cr, None)

    def guarded(d, act):
        if exists[d] is None:
            act()
        else:
            pl.when(exists[d])(act)

    def neighbour(src, dst, send, recv, d):
        return pltpu.make_async_remote_copy(
            src_ref=src, dst_ref=dst.at[3 - d], send_sem=send, recv_sem=recv,
            device_id=device[d], device_id_type=LOGICAL,
        )

    def halo_copy(stage, d):
        return neighbour(own.at[stage], halo.at[stage], halo_send.at[d], halo_recv.at[stage], d)

    def ret_copy(it, d):
        src = ret_out.at[it, pl.ds(PLACES[d] * blocks, blocks)]
        return neighbour(src, ret_in.at[it], ret_send.at[d], ret_recv.at[it], d)

    def rows_copy(d):
        return neighbour(rows_out.at[d], rows_in, rows_send.at[d], rows_recv.at[3 - d], d)

    def wait_for(ref, sem):
        pltpu.make_async_copy(ref, ref, sem).wait()

    inner = exists[1] & exists[2]

    def arrived_all(ref, sem):
        @pl.when(inner)
        def _():
            wait_for(ref, sem)

        @pl.when(jnp.logical_not(inner))
        def _():
            wait_for(ref.at[pl.ds(0, 3)], sem)

    def ax_copy(it, step):
        return pltpu.make_async_remote_copy(
            src_ref=part_ax.at[it, me_a], dst_ref=part_ax.at[it, me_a],
            send_sem=ax_send, recv_sem=ax_recv.at[it],
            device_id=ax_peer(step), device_id_type=LOGICAL,
        )

    def cr_copy(it, step):
        return pltpu.make_async_remote_copy(
            src_ref=part_cr.at[it, me_c], dst_ref=part_cr.at[it, me_c],
            send_sem=cr_send, recv_sem=cr_recv.at[it],
            device_id=cr_peer(step), device_id_type=LOGICAL,
        )

    fetched = (
        (force_hbm, force_ref), (ids_hbm, ids_ref), (count_hbm, count_ref),
        (drag_hbm, drag_ref), (rows_hbm, rows_ref),
    )
    small = [pltpu.make_async_copy(a, b, small_sem.at[n]) for n, (a, b) in enumerate(fetched)]
    for copy in small:
        copy.start()

    barrier = pltpu.get_barrier_semaphore()
    for step in range(1, n_ax):
        pl.semaphore_signal(barrier, inc=1, device_id=ax_peer(step), device_id_type=LOGICAL)
    for step in range(1, n_cr):
        pl.semaphore_signal(barrier, inc=1, device_id=cr_peer(step), device_id_type=LOGICAL)

    load = pltpu.make_async_copy(tiles_ref, tile_buf, tile_sem)
    load.start()
    for copy in small:
        copy.wait()

    force = jnp.concatenate([force_ref[c] for c in range(3)], axis=1)
    own[0] = force
    lane = lax.broadcasted_iota(jnp.int32, (1, 128), 1)
    mig[0:2, 0:slot] = rows_ref[...]
    listed = mig[...]
    turned = pltpu.roll(listed, 64, 1)
    rows_out[1] = jnp.where((lane < slot) & (lane < count_ref[0]), listed[0:1], -1)
    rows_out[2] = jnp.where((lane >= 64) & (lane - 64 < count_ref[1]), turned[1:2], -1)

    for d in (1, 2):
        @pl.when(jnp.logical_not(exists[d]))
        def _():
            for stage in range(ITERS):
                halo[stage, d] = jnp.zeros((blocks, 3 * width), F32)
                ret_in[stage, d] = jnp.zeros((blocks, 3 * width), F32)
            rows_in[d] = jnp.full((1, 128), -1, jnp.int32)

    pl.semaphore_wait(barrier, n_ax - 1 + n_cr - 1)

    for d in range(4):
        guarded(d, lambda d=d: halo_copy(0, d).start())
    for d in (1, 2):
        guarded(d, lambda d=d: rows_copy(d).start())

    ext[...] = jnp.zeros(ext.shape, F32)
    wide = lax.broadcasted_iota(jnp.int32, (1, 2 * pairs), 1)
    listed_ids = jnp.zeros((1, 2 * pairs), jnp.int32)
    for n in range(pairs):
        hit = (wide == n) | (wide == n + pairs)
        listed_ids = jnp.where(hit, ids_ref[n // count, n % count], listed_ids)
    entry = lax.broadcasted_iota(jnp.int32, (8 * blocks, 2 * pairs), 0)
    selector = jnp.where(entry == listed_ids, 1.0, 0.0).astype(BF16)
    drag = drag_ref[...]
    drag3 = jnp.concatenate([drag] * 3, axis=1)

    def place(p, field):
        for c, part in enumerate(chunks(field)):
            ext[p * blocks:(p + 1) * blocks, c, :] = part

    def tile_row(b):
        return jnp.concatenate([tile_buf[b, k] for k in range(count)], axis=1)

    def total(parts):
        return jnp.sum(functools.reduce(jnp.add, parts), axis=0, keepdims=True)

    place(CENTRE, force)
    residual = force
    velocity = direction = image = None
    near = [None] * 4
    near_image = [None] * 4
    near_velocity = [None] * 4
    near_direction = [None] * 4
    track = [None] * blocks
    norm_before = energy_before = None

    load.wait()
    for b in range(blocks):
        for k in range(count):
            side = (b % 2) * width
            tile_turned[b // 2, k * width:(k + 1) * width, side:side + width] = tile_buf[b, k].T
    arrived_all(halo.at[0], halo_recv.at[0])
    for d in range(4):
        near[d] = halo[0, d]

    for it in range(ITERS):
        last = it == ITERS - 1
        if it:
            place(CENTRE, residual)
        for d in range(4):
            place(PLACES[d], near[d])
        coupled = []
        for b in range(0, blocks, 2):
            picked = jnp.concatenate([
                jnp.concatenate([ext[ids_ref[b + s, k]] for k in range(count)], axis=1) for s in range(2)
            ], axis=0)
            pair = jnp.dot(picked.astype(BF16), tile_turned[b // 2], preferred_element_type=F32)
            coupled += [pair[0:8, 0:width], pair[8:16, width:2 * width]]

        square = functools.reduce(jnp.add, chunks(residual * residual))
        sums = [
            jnp.sum(square, axis=0, keepdims=True),
            total([drag * square] + [c * c for c in coupled]),
        ]
        if it:
            mixed = functools.reduce(jnp.add, chunks(residual * direction))
            sums.append(total([drag * mixed] + [c * t for c, t in zip(coupled, track)]))
        else:
            sums.append(jnp.zeros((1, 128), F32))
        part_ax[it, me_a] = jnp.concatenate(sums, axis=1)
        for step in range(1, n_ax):
            ax_copy(it, step).start()

        for b in range(0, blocks, 2):
            blank = jnp.zeros((8, width), F32)
            diagonal = jnp.concatenate([
                jnp.concatenate([coupled[b], blank], axis=1),
                jnp.concatenate([blank, coupled[b + 1]], axis=1),
            ], axis=0)
            both = jnp.concatenate([tile_row(b), tile_row(b + 1)], axis=0)
            back = jnp.dot(diagonal.astype(BF16), both, preferred_element_type=F32)
            for k in range(count):
                spread[pl.ds((b * count + k) * 8, 8), :] = back[0:8, k * width:(k + 1) * width]
                spread[pl.ds(((b + 1) * count + k) * 8, 8), :] = back[8:16, k * width:(k + 1) * width]
        listed_spread = jnp.concatenate([spread[pl.ds(c, pairs, 8), :] for c in range(3)], axis=1)
        high = listed_spread.astype(BF16)
        low = (listed_spread - high.astype(F32)).astype(BF16)
        ret_out[it] = jnp.dot(
            selector, jnp.concatenate([high, low], axis=0), preferred_element_type=F32
        )
        for d in range(4):
            guarded(d, lambda d=d: ret_copy(it, d).start())

        wait_for(part_ax.at[it, pl.ds(0, n_ax - 1)], ax_recv.at[it])
        part_cr[it, me_c] = functools.reduce(jnp.add, [part_ax[it, i] for i in range(n_ax)])
        for step in range(1, n_cr):
            cr_copy(it, step).start()

        if last:
            gathered = [0.0] * 9
            for d in (1, 2):
                guarded(d, lambda d=d: wait_for(rows_in.at[d], rows_recv.at[d]))
                rows = rows_in[d]
                fields = [near_velocity[d], near[d], near_direction[d]]
                stack = jnp.concatenate([part for f in fields for part in chunks(f)], axis=0)
                first = stack.astype(BF16)
                rest = stack - first.astype(F32)
                second = rest.astype(BF16)
                third = (rest - second.astype(F32)).astype(BF16)
                bead = lax.broadcasted_iota(jnp.int32, (width, 128), 0)
                onehot = jnp.where(bead == (rows & (width - 1)), 1.0, 0.0).astype(BF16)
                found = sum(
                    jnp.dot(piece, onehot, preferred_element_type=F32) for piece in (third, second, first)
                )
                block = lax.broadcasted_iota(jnp.int32, (blocks, 128), 0)
                mine = block == (rows >> (width.bit_length() - 1))
                for n in range(9):
                    part = jnp.where(mine, found[n * blocks:(n + 1) * blocks], 0.0)
                    gathered[n] = gathered[n] + jnp.sum(part, axis=0, keepdims=True)

        arrived_all(ret_in.at[it], ret_recv.at[it])
        product = drag3 * residual + ret_out[it, CENTRE * blocks:(CENTRE + 1) * blocks]
        for d in range(4):
            product = product + ret_in[it, d]
        if not last:
            own[it + 1] = product
            for d in range(4):
                guarded(d, lambda d=d: halo_copy(it + 1, d).start())

        wait_for(part_cr.at[it, pl.ds(0, n_cr - 1)], cr_recv.at[it])
        summed = functools.reduce(jnp.add, [part_cr[it, i] for i in range(n_cr)])
        norm, energy, cross = [jnp.sum(s, axis=1, keepdims=True) for s in chunks(summed)]
        if it:
            beta = norm / norm_before
            energy = energy + 2.0 * beta * cross + beta * beta * energy_before
        alpha = norm / energy
        norm_before, energy_before = norm, energy

        def follow(now, before):
            return now + beta * before if it else now

        image = follow(product, image)
        direction = follow(residual, direction)
        velocity = velocity + alpha * direction if it else alpha * direction
        residual = residual - alpha * image
        if last:
            break
        track = [follow(c, t) for c, t in zip(coupled, track)]
        arrived_all(halo.at[it + 1], halo_recv.at[it + 1])
        for d in range(4):
            near_image[d] = follow(halo[it + 1, d], near_image[d])
            if d in (1, 2):
                near_direction[d] = follow(near[d], near_direction[d])
                step_v = alpha * near_direction[d]
                near_velocity[d] = near_velocity[d] + step_v if it else step_v
            near[d] = near[d] - alpha * near_image[d]

    for c in range(3):
        vel_ref[c] = chunks(velocity)[c]
        res_ref[c] = chunks(residual)[c]
    for c in range(3):
        row = gathered[c] + alpha * (gathered[3 + c] + beta * gathered[6 + c])
        arr_ref[c] = pltpu.roll(row, 64, 1)

    for d in (1, 2):
        guarded(d, lambda d=d: wait_for(rows_out.at[d], rows_send.at[d]))
    for d in range(4):
        guarded(d, lambda d=d: wait_for(own, halo_send.at[d]))
        guarded(d, lambda d=d: wait_for(own, ret_send.at[d]))
    wait_for(part_ax.at[:, pl.ds(0, n_ax - 1)], ax_send)
    wait_for(part_cr.at[:, pl.ds(0, n_cr - 1)], cr_send)


def write_out(vel_in, res_in, arr_in, vel_ref, res_ref, arr_ref, sem):
    moves = ((vel_in, vel_ref), (res_in, res_ref), (arr_in, arr_ref))
    copies = [pltpu.make_async_copy(a, b, sem.at[n]) for n, (a, b) in enumerate(moves)]
    for copy in copies:
        copy.start()
    for copy in copies:
        copy.wait()


def on_device(n_ax, n_cr, force, self_drag, tiles, tile_ids, mig_rows, mig_count):
    blocks, width = force.shape[2], force.shape[4]
    count = tiles.shape[3]
    field = (blocks, 3 * width)
    vmem = pl.BlockSpec(memory_space=pltpu.VMEM)
    dma = pltpu.SemaphoreType.DMA
    hbm = pl.BlockSpec(memory_space=pltpu.HBM)
    solved = pl.pallas_call(
        functools.partial(kernel, n_ax, n_cr),
        out_shape=(
            pltpu.VMEM((3, blocks, width), F32),
            pltpu.VMEM((3, blocks, width), F32),
            pltpu.VMEM((3, 1, 2 * mig_rows.shape[3]), F32),
        ),
        in_specs=[hbm] * 6,
        out_specs=(vmem, vmem, vmem),
        scratch_shapes=[
            pltpu.SMEM((blocks, count), jnp.int32),
            pltpu.SMEM((2,), jnp.int32),
            pltpu.VMEM((3, blocks, width), F32),
            pltpu.VMEM((blocks, width), F32),
            pltpu.VMEM(mig_rows.shape[2:], jnp.int32),
            pltpu.VMEM((blocks, count, width, width), BF16),
            pltpu.VMEM((blocks // 2, count * width, 2 * width), BF16),
            pltpu.VMEM((8 * blocks, 8, width), F32),
            pltpu.VMEM((blocks * count * 8, width), F32),
            pltpu.VMEM((ITERS,) + field, F32),
            pltpu.VMEM((ITERS, 4) + field, F32),
            pltpu.VMEM((ITERS, 8 * blocks, 3 * width), F32),
            pltpu.VMEM((ITERS, 4) + field, F32),
            pltpu.VMEM((ITERS, n_ax, 1, 384), F32),
            pltpu.VMEM((ITERS, n_cr, 1, 384), F32),
            pltpu.VMEM((8, 128), jnp.int32),
            pltpu.VMEM((3, 1, 128), jnp.int32),
            pltpu.VMEM((3, 1, 128), jnp.int32),
            dma, dma((5,)),
            dma((4,)), dma((ITERS,)),
            dma((4,)), dma((ITERS,)),
            dma((3,)), dma((3,)),
            dma, dma((ITERS,)),
            dma, dma((ITERS,)),
        ],
        compiler_params=pltpu.CompilerParams(
            collective_id=0, has_side_effects=True, vmem_limit_bytes=60 * 1024 * 1024
        ),
        name="cg_solve",
    )(
        tile_ids.reshape(tile_ids.shape[2:]),
        mig_count.reshape(mig_count.shape[2:]),
        jnp.swapaxes(force[0, 0], 0, 1),
        self_drag.reshape(self_drag.shape[2:]),
        tiles.reshape(tiles.shape[2:]),
        mig_rows.reshape(mig_rows.shape[2:]),
    )
    velocity, residual, arrivals = pl.pallas_call(
        write_out,
        out_shape=tuple(jax.ShapeDtypeStruct(x.shape, x.dtype) for x in solved),
        in_specs=[vmem] * 3,
        out_specs=(hbm,) * 3,
        scratch_shapes=[dma((3,))],
        compiler_params=pltpu.CompilerParams(vmem_limit_bytes=1024 * 1024),
        name="write_out",
    )(*solved)
    velocity, residual = jnp.swapaxes(velocity, 0, 1), jnp.swapaxes(residual, 0, 1)
    return velocity[None, None], residual[None, None], arrivals[:, 0][None, None]


def solution(mesh):
    placed = (
        P("axial", "cross", None, None, None),
        P("axial", "cross", None, None),
        P("axial", "cross", None, None, None, None),
        P("axial", "cross", None, None),
        P("axial", "cross", None, None),
        P("axial", "cross", None),
    )
    return jax.shard_map(
        functools.partial(on_device, mesh.shape["axial"], mesh.shape["cross"]),
        mesh=mesh,
        in_specs=placed,
        out_specs=(
            P("axial", "cross", None, None, None),
            P("axial", "cross", None, None, None),
            P("axial", "cross", None, None),
        ),
        check_vma=False,
    )
```

```python
import functools

import jax
import jax.numpy as jnp
from jax import lax
from jax.experimental import pallas as pl
from jax.experimental.pallas import tpu as pltpu
from jax.sharding import PartitionSpec as P

ITERS = 3
LOGICAL = pl.DeviceIdType.LOGICAL
PLACES = (1, 3, 5, 7)
CENTRE = 4
F32 = jnp.float32
BF16 = jnp.bfloat16


def chunks(field):
    return [field[:, c * 128:(c + 1) * 128] for c in range(3)]


def kernel(
    n_ax, n_cr,
    ids_hbm, count_hbm, force_hbm, drag_hbm, tiles_ref, rows_hbm,
    vel_ref, res_ref, arr_ref,
    ids_ref, count_ref, force_ref, drag_ref, rows_ref, tile_buf, tile_turned, ext, spread, own, halo, ret_out, ret_in, parts, mig, rows_out, rows_in,
    tile_sem, small_sem, halo_send, halo_recv, ret_send, ret_recv, rows_send, rows_recv,
    sum_send, sum_recv,
):
    blocks, count, width = tiles_ref.shape[0], tiles_ref.shape[1], tiles_ref.shape[2]
    pairs = blocks * count
    slot = rows_hbm.shape[1]
    me_a = lax.axis_index("axial")
    me_c = lax.axis_index("cross")

    me = me_a * n_cr + me_c
    device = (
        jnp.where(me_a > 0, me - n_cr, me + (n_ax - 1) * n_cr),
        me - 1,
        me + 1,
        jnp.where(me_a + 1 < n_ax, me + n_cr, me - (n_ax - 1) * n_cr),
    )
    exists = (None, me_c > 0, me_c + 1 < n_cr, None)

    def guarded(d, act):
        if exists[d] is None:
            act()
        else:
            pl.when(exists[d])(act)

    def neighbour(src, dst, send, recv, d):
        return pltpu.make_async_remote_copy(
            src_ref=src, dst_ref=dst.at[3 - d], send_sem=send, recv_sem=recv,
            device_id=device[d], device_id_type=LOGICAL,
        )

    def halo_copy(stage, d):
        return neighbour(own.at[stage], halo.at[stage], halo_send.at[d], halo_recv.at[stage], d)

    def ret_copy(it, d):
        src = ret_out.at[it, pl.ds(PLACES[d] * blocks, blocks)]
        return neighbour(src, ret_in.at[it], ret_send.at[d], ret_recv.at[it], d)

    def rows_copy(d):
        return neighbour(rows_out.at[d], rows_in, rows_send.at[d], rows_recv.at[3 - d], d)

    def wait_for(ref, sem):
        pltpu.make_async_copy(ref, ref, sem).wait()

    inner = exists[1] & exists[2]

    def arrived_all(ref, sem):
        @pl.when(inner)
        def _():
            wait_for(ref, sem)

        @pl.when(jnp.logical_not(inner))
        def _():
            wait_for(ref.at[pl.ds(0, 3)], sem)

    everyone = n_ax * n_cr

    def peer(step):
        return jnp.where(me + step < everyone, me + step, me + step - everyone)

    def sum_copy(it, step):
        return pltpu.make_async_remote_copy(
            src_ref=parts.at[it, me], dst_ref=parts.at[it, me],
            send_sem=sum_send, recv_sem=sum_recv.at[it],
            device_id=peer(step), device_id_type=LOGICAL,
        )

    def each_peer(act):
        def body(step, carry):
            act(step)
            return carry
        lax.fori_loop(1, everyone, body, 0)

    fetched = (
        (force_hbm, force_ref), (ids_hbm, ids_ref), (count_hbm, count_ref),
        (drag_hbm, drag_ref), (rows_hbm, rows_ref),
    )
    small = [pltpu.make_async_copy(a, b, small_sem.at[n]) for n, (a, b) in enumerate(fetched)]
    for copy in small:
        copy.start()

    barrier = pltpu.get_barrier_semaphore()
    each_peer(lambda step: pl.semaphore_signal(barrier, inc=1, device_id=peer(step), device_id_type=LOGICAL))

    load = pltpu.make_async_copy(tiles_ref, tile_buf, tile_sem)
    load.start()
    for copy in small:
        copy.wait()

    force = jnp.concatenate([force_ref[c] for c in range(3)], axis=1)
    own[0] = force
    lane = lax.broadcasted_iota(jnp.int32, (1, 128), 1)
    mig[0:2, 0:slot] = rows_ref[...]
    listed = mig[...]
    turned = pltpu.roll(listed, 64, 1)
    rows_out[1] = jnp.where((lane < slot) & (lane < count_ref[0]), listed[0:1], -1)
    rows_out[2] = jnp.where((lane >= 64) & (lane - 64 < count_ref[1]), turned[1:2], -1)

    for d in (1, 2):
        @pl.when(jnp.logical_not(exists[d]))
        def _():
            for stage in range(ITERS):
                halo[stage, d] = jnp.zeros((blocks, 3 * width), F32)
                ret_in[stage, d] = jnp.zeros((blocks, 3 * width), F32)
            rows_in[d] = jnp.full((1, 128), -1, jnp.int32)

    pl.semaphore_wait(barrier, everyone - 1)

    for d in range(4):
        guarded(d, lambda d=d: halo_copy(0, d).start())
    for d in (1, 2):
        guarded(d, lambda d=d: rows_copy(d).start())

    ext[...] = jnp.zeros(ext.shape, F32)
    wide = lax.broadcasted_iota(jnp.int32, (1, 2 * pairs), 1)
    listed_ids = jnp.zeros((1, 2 * pairs), jnp.int32)
    for n in range(pairs):
        hit = (wide == n) | (wide == n + pairs)
        listed_ids = jnp.where(hit, ids_ref[n // count, n % count], listed_ids)
    entry = lax.broadcasted_iota(jnp.int32, (8 * blocks, 2 * pairs), 0)
    selector = jnp.where(entry == listed_ids, 1.0, 0.0).astype(BF16)
    drag = drag_ref[...]
    drag3 = jnp.concatenate([drag] * 3, axis=1)

    def place(p, field):
        for c, part in enumerate(chunks(field)):
            ext[p * blocks:(p + 1) * blocks, c, :] = part

    def tile_row(b):
        return jnp.concatenate([tile_buf[b, k] for k in range(count)], axis=1)

    def total(parts):
        return jnp.sum(functools.reduce(jnp.add, parts), axis=0, keepdims=True)

    place(CENTRE, force)
    residual = force
    velocity = direction = image = None
    near = [None] * 4
    near_image = [None] * 4
    near_velocity = [None] * 4
    near_direction = [None] * 4
    track = [None] * blocks
    norm_before = energy_before = None

    load.wait()
    for b in range(blocks):
        for k in range(count):
            side = (b % 2) * width
            tile_turned[b // 2, k * width:(k + 1) * width, side:side + width] = tile_buf[b, k].T
    arrived_all(halo.at[0], halo_recv.at[0])
    for d in range(4):
        near[d] = halo[0, d]

    for it in range(ITERS):
        last = it == ITERS - 1
        if it:
            place(CENTRE, residual)
        for d in range(4):
            place(PLACES[d], near[d])
        coupled = []
        for b in range(0, blocks, 2):
            picked = jnp.concatenate([
                jnp.concatenate([ext[ids_ref[b + s, k]] for k in range(count)], axis=1) for s in range(2)
            ], axis=0)
            pair = jnp.dot(picked.astype(BF16), tile_turned[b // 2], preferred_element_type=F32)
            coupled += [pair[0:8, 0:width], pair[8:16, width:2 * width]]

        square = functools.reduce(jnp.add, chunks(residual * residual))
        sums = [
            jnp.sum(square, axis=0, keepdims=True),
            total([drag * square] + [c * c for c in coupled]),
        ]
        if it:
            mixed = functools.reduce(jnp.add, chunks(residual * direction))
            sums.append(total([drag * mixed] + [c * t for c, t in zip(coupled, track)]))
        else:
            sums.append(jnp.zeros((1, 128), F32))
        packed = jnp.zeros((1, 128), F32)
        for n, row in enumerate(sums):
            packed = jnp.where(lane == n, jnp.sum(row, axis=1, keepdims=True), packed)
        parts[it, me] = packed
        each_peer(lambda step: sum_copy(it, step).start())

        for b in range(0, blocks, 2):
            blank = jnp.zeros((8, width), F32)
            diagonal = jnp.concatenate([
                jnp.concatenate([coupled[b], blank], axis=1),
                jnp.concatenate([blank, coupled[b + 1]], axis=1),
            ], axis=0)
            both = jnp.concatenate([tile_row(b), tile_row(b + 1)], axis=0)
            back = jnp.dot(diagonal.astype(BF16), both, preferred_element_type=F32)
            for k in range(count):
                spread[pl.ds((b * count + k) * 8, 8), :] = back[0:8, k * width:(k + 1) * width]
                spread[pl.ds(((b + 1) * count + k) * 8, 8), :] = back[8:16, k * width:(k + 1) * width]
        listed_spread = jnp.concatenate([spread[pl.ds(c, pairs, 8), :] for c in range(3)], axis=1)
        high = listed_spread.astype(BF16)
        low = (listed_spread - high.astype(F32)).astype(BF16)
        ret_out[it] = jnp.dot(
            selector, jnp.concatenate([high, low], axis=0), preferred_element_type=F32
        )
        for d in range(4):
            guarded(d, lambda d=d: ret_copy(it, d).start())

        if last:
            gathered = [0.0] * 9
            for d in (1, 2):
                guarded(d, lambda d=d: wait_for(rows_in.at[d], rows_recv.at[d]))
                rows = rows_in[d]
                fields = [near_velocity[d], near[d], near_direction[d]]
                stack = jnp.concatenate([part for f in fields for part in chunks(f)], axis=0)
                first = stack.astype(BF16)
                rest = stack - first.astype(F32)
                second = rest.astype(BF16)
                third = (rest - second.astype(F32)).astype(BF16)
                bead = lax.broadcasted_iota(jnp.int32, (width, 128), 0)
                onehot = jnp.where(bead == (rows & (width - 1)), 1.0, 0.0).astype(BF16)
                found = sum(
                    jnp.dot(piece, onehot, preferred_element_type=F32) for piece in (third, second, first)
                )
                block = lax.broadcasted_iota(jnp.int32, (blocks, 128), 0)
                mine = block == (rows >> (width.bit_length() - 1))
                for n in range(9):
                    part = jnp.where(mine, found[n * blocks:(n + 1) * blocks], 0.0)
                    gathered[n] = gathered[n] + jnp.sum(part, axis=0, keepdims=True)

        arrived_all(ret_in.at[it], ret_recv.at[it])
        product = drag3 * residual + ret_out[it, CENTRE * blocks:(CENTRE + 1) * blocks]
        for d in range(4):
            product = product + ret_in[it, d]
        if not last:
            own[it + 1] = product
            for d in range(4):
                guarded(d, lambda d=d: halo_copy(it + 1, d).start())

        wait_for(parts.at[it, pl.ds(0, everyone - 1)], sum_recv.at[it])
        summed = jnp.sum(parts[it], axis=0)
        norm, energy, cross = [
            jnp.sum(jnp.where(lane == n, summed, 0.0), axis=1, keepdims=True) for n in range(3)
        ]
        if it:
            beta = norm / norm_before
            energy = energy + 2.0 * beta * cross + beta * beta * energy_before
        alpha = norm / energy
        norm_before, energy_before = norm, energy

        def follow(now, before):
            return now + beta * before if it else now

        image = follow(product, image)
        direction = follow(residual, direction)
        velocity = velocity + alpha * direction if it else alpha * direction
        residual = residual - alpha * image
        if last:
            break
        track = [follow(c, t) for c, t in zip(coupled, track)]
        arrived_all(halo.at[it + 1], halo_recv.at[it + 1])
        for d in range(4):
            near_image[d] = follow(halo[it + 1, d], near_image[d])
            if d in (1, 2):
                near_direction[d] = follow(near[d], near_direction[d])
                step_v = alpha * near_direction[d]
                near_velocity[d] = near_velocity[d] + step_v if it else step_v
            near[d] = near[d] - alpha * near_image[d]

    for c in range(3):
        vel_ref[c] = chunks(velocity)[c]
        res_ref[c] = chunks(residual)[c]
    for c in range(3):
        row = gathered[c] + alpha * (gathered[3 + c] + beta * gathered[6 + c])
        arr_ref[c] = pltpu.roll(row, 64, 1)

    for d in (1, 2):
        guarded(d, lambda d=d: wait_for(rows_out.at[d], rows_send.at[d]))
    for d in range(4):
        guarded(d, lambda d=d: wait_for(own, halo_send.at[d]))
        guarded(d, lambda d=d: wait_for(own, ret_send.at[d]))
    wait_for(parts.at[:, pl.ds(0, everyone - 1)], sum_send)


def write_out(vel_in, res_in, arr_in, vel_ref, res_ref, arr_ref, sem):
    moves = ((vel_in, vel_ref), (res_in, res_ref), (arr_in, arr_ref))
    copies = [pltpu.make_async_copy(a, b, sem.at[n]) for n, (a, b) in enumerate(moves)]
    for copy in copies:
        copy.start()
    for copy in copies:
        copy.wait()


def on_device(n_ax, n_cr, force, self_drag, tiles, tile_ids, mig_rows, mig_count):
    blocks, width = force.shape[2], force.shape[4]
    count = tiles.shape[3]
    field = (blocks, 3 * width)
    vmem = pl.BlockSpec(memory_space=pltpu.VMEM)
    dma = pltpu.SemaphoreType.DMA
    hbm = pl.BlockSpec(memory_space=pltpu.HBM)
    solved = pl.pallas_call(
        functools.partial(kernel, n_ax, n_cr),
        out_shape=(
            pltpu.VMEM((3, blocks, width), F32),
            pltpu.VMEM((3, blocks, width), F32),
            pltpu.VMEM((3, 1, 2 * mig_rows.shape[3]), F32),
        ),
        in_specs=[hbm] * 6,
        out_specs=(vmem, vmem, vmem),
        scratch_shapes=[
            pltpu.SMEM((blocks, count), jnp.int32),
            pltpu.SMEM((2,), jnp.int32),
            pltpu.VMEM((3, blocks, width), F32),
            pltpu.VMEM((blocks, width), F32),
            pltpu.VMEM(mig_rows.shape[2:], jnp.int32),
            pltpu.VMEM((blocks, count, width, width), BF16),
            pltpu.VMEM((blocks // 2, count * width, 2 * width), BF16),
            pltpu.VMEM((8 * blocks, 8, width), F32),
            pltpu.VMEM((blocks * count * 8, width), F32),
            pltpu.VMEM((ITERS,) + field, F32),
            pltpu.VMEM((ITERS, 4) + field, F32),
            pltpu.VMEM((ITERS, 8 * blocks, 3 * width), F32),
            pltpu.VMEM((ITERS, 4) + field, F32),
            pltpu.VMEM((ITERS, n_ax * n_cr, 1, 128), F32),
            pltpu.VMEM((8, 128), jnp.int32),
            pltpu.VMEM((3, 1, 128), jnp.int32),
            pltpu.VMEM((3, 1, 128), jnp.int32),
            dma, dma((5,)),
            dma((4,)), dma((ITERS,)),
            dma((4,)), dma((ITERS,)),
            dma((3,)), dma((3,)),
            dma, dma((ITERS,)),
        ],
        compiler_params=pltpu.CompilerParams(
            collective_id=0, has_side_effects=True, vmem_limit_bytes=60 * 1024 * 1024
        ),
        name="cg_solve",
    )(
        tile_ids.reshape(tile_ids.shape[2:]),
        mig_count.reshape(mig_count.shape[2:]),
        jnp.swapaxes(force[0, 0], 0, 1),
        self_drag.reshape(self_drag.shape[2:]),
        tiles.reshape(tiles.shape[2:]),
        mig_rows.reshape(mig_rows.shape[2:]),
    )
    velocity, residual, arrivals = pl.pallas_call(
        write_out,
        out_shape=tuple(jax.ShapeDtypeStruct(x.shape, x.dtype) for x in solved),
        in_specs=[vmem] * 3,
        out_specs=(hbm,) * 3,
        scratch_shapes=[dma((3,))],
        compiler_params=pltpu.CompilerParams(vmem_limit_bytes=1024 * 1024),
        name="write_out",
    )(*solved)
    velocity, residual = jnp.swapaxes(velocity, 0, 1), jnp.swapaxes(residual, 0, 1)
    return velocity[None, None], residual[None, None], arrivals[:, 0][None, None]


def solution(mesh):
    placed = (
        P("axial", "cross", None, None, None),
        P("axial", "cross", None, None),
        P("axial", "cross", None, None, None, None),
        P("axial", "cross", None, None),
        P("axial", "cross", None, None),
        P("axial", "cross", None),
    )
    return jax.shard_map(
        functools.partial(on_device, mesh.shape["axial"], mesh.shape["cross"]),
        mesh=mesh,
        in_specs=placed,
        out_specs=(
            P("axial", "cross", None, None, None),
            P("axial", "cross", None, None, None),
            P("axial", "cross", None, None),
        ),
        check_vma=False,
    )
```

```python
import functools

import jax
import jax.numpy as jnp
from jax import lax
from jax.experimental import pallas as pl
from jax.experimental.pallas import tpu as pltpu
from jax.sharding import PartitionSpec as P

ITERS = 3
LOGICAL = pl.DeviceIdType.LOGICAL
PLACES = (1, 3, 5, 7)
CENTRE = 4
F32 = jnp.float32
BF16 = jnp.bfloat16


def chunks(field):
    return [field[:, c * 128:(c + 1) * 128] for c in range(3)]


def kernel(
    n_ax, n_cr,
    ids_hbm, count_hbm, force_hbm, drag_hbm, tiles_ref, rows_hbm,
    vel_ref, res_ref, arr_ref,
    ids_ref, count_ref, force_ref, drag_ref, rows_ref, tile_buf, tile_turned, ext, spread, own, halo, ret_out, ret_in, parts, mig, rows_out, rows_in,
    tile_sem, small_sem, halo_send, halo_recv, ret_send, ret_recv, rows_send, rows_recv,
    sum_send, sum_recv,
):
    blocks, count, width = tiles_ref.shape[0], tiles_ref.shape[1], tiles_ref.shape[2]
    pairs = blocks * count
    slot = rows_hbm.shape[1]
    me_a = lax.axis_index("axial")
    me_c = lax.axis_index("cross")

    me = me_a * n_cr + me_c
    device = (
        jnp.where(me_a > 0, me - n_cr, me + (n_ax - 1) * n_cr),
        me - 1,
        me + 1,
        jnp.where(me_a + 1 < n_ax, me + n_cr, me - (n_ax - 1) * n_cr),
    )
    exists = (None, me_c > 0, me_c + 1 < n_cr, None)

    def guarded(d, act):
        if exists[d] is None:
            act()
        else:
            pl.when(exists[d])(act)

    def neighbour(src, dst, send, recv, d):
        return pltpu.make_async_remote_copy(
            src_ref=src, dst_ref=dst.at[3 - d], send_sem=send, recv_sem=recv,
            device_id=device[d], device_id_type=LOGICAL,
        )

    def halo_copy(stage, d):
        return neighbour(own.at[stage], halo.at[stage], halo_send.at[d], halo_recv.at[stage], d)

    def ret_copy(it, d):
        src = ret_out.at[it, pl.ds(PLACES[d] * blocks, blocks)]
        return neighbour(src, ret_in.at[it], ret_send.at[d], ret_recv.at[it], d)

    def rows_copy(d):
        return neighbour(rows_out.at[d], rows_in, rows_send.at[d], rows_recv.at[3 - d], d)

    def wait_for(ref, sem):
        pltpu.make_async_copy(ref, ref, sem).wait()

    inner = exists[1] & exists[2]

    def arrived_all(ref, sem):
        @pl.when(inner)
        def _():
            wait_for(ref, sem)

        @pl.when(jnp.logical_not(inner))
        def _():
            wait_for(ref.at[pl.ds(0, 3)], sem)

    everyone = n_ax * n_cr

    def peer(step):
        return jnp.where(me + step < everyone, me + step, me + step - everyone)

    def sum_copy(it, step):
        return pltpu.make_async_remote_copy(
            src_ref=parts.at[it, me], dst_ref=parts.at[it, me],
            send_sem=sum_send, recv_sem=sum_recv.at[it],
            device_id=peer(step), device_id_type=LOGICAL,
        )

    def each_peer(act):
        def body(step, carry):
            act(step)
            return carry
        lax.fori_loop(1, everyone, body, 0)

    fetched = (
        (force_hbm, force_ref), (ids_hbm, ids_ref), (count_hbm, count_ref),
        (drag_hbm, drag_ref), (rows_hbm, rows_ref),
    )
    small = [pltpu.make_async_copy(a, b, small_sem.at[n]) for n, (a, b) in enumerate(fetched)]
    for copy in small:
        copy.start()

    barrier = pltpu.get_barrier_semaphore()
    each_peer(lambda step: pl.semaphore_signal(barrier, inc=1, device_id=peer(step), device_id_type=LOGICAL))

    load = pltpu.make_async_copy(tiles_ref, tile_buf, tile_sem)
    load.start()
    for copy in small:
        copy.wait()

    force = jnp.concatenate([force_ref[c] for c in range(3)], axis=1)
    own[0] = force
    lane = lax.broadcasted_iota(jnp.int32, (1, 128), 1)
    mig[0:2, 0:slot] = rows_ref[...]
    listed = mig[...]
    turned = pltpu.roll(listed, 64, 1)
    rows_out[1] = jnp.where((lane < slot) & (lane < count_ref[0]), listed[0:1], -1)
    rows_out[2] = jnp.where((lane >= 64) & (lane - 64 < count_ref[1]), turned[1:2], -1)

    for d in (1, 2):
        @pl.when(jnp.logical_not(exists[d]))
        def _():
            for stage in range(ITERS):
                halo[stage, d] = jnp.zeros((blocks, 3 * width), F32)
                ret_in[stage, d] = jnp.zeros((blocks, 3 * width), F32)
            rows_in[d] = jnp.full((1, 128), -1, jnp.int32)

    pl.semaphore_wait(barrier, everyone - 1)

    for d in range(4):
        guarded(d, lambda d=d: halo_copy(0, d).start())
    for d in (1, 2):
        guarded(d, lambda d=d: rows_copy(d).start())

    ext[...] = jnp.zeros(ext.shape, F32)
    wide = lax.broadcasted_iota(jnp.int32, (1, 2 * pairs), 1)
    listed_ids = jnp.zeros((1, 2 * pairs), jnp.int32)
    for n in range(pairs):
        hit = (wide == n) | (wide == n + pairs)
        listed_ids = jnp.where(hit, ids_ref[n // count, n % count], listed_ids)
    entry = lax.broadcasted_iota(jnp.int32, (8 * blocks, 2 * pairs), 0)
    selector = jnp.where(entry == listed_ids, 1.0, 0.0).astype(BF16)
    drag = drag_ref[...]
    drag3 = jnp.concatenate([drag] * 3, axis=1)

    def place(p, field):
        for c, part in enumerate(chunks(field)):
            ext[p * blocks:(p + 1) * blocks, c, :] = part

    def tile_row(b):
        return jnp.concatenate([tile_buf[b, k] for k in range(count)], axis=1)

    def total(parts):
        return jnp.sum(functools.reduce(jnp.add, parts), axis=0, keepdims=True)

    place(CENTRE, force)
    residual = force
    velocity = direction = image = None
    near = [None] * 4
    near_image = [None] * 4
    near_velocity = [None] * 4
    near_direction = [None] * 4
    track = [None] * blocks
    norm_before = energy_before = None

    load.wait()
    for b in range(blocks):
        for k in range(count):
            side = (b % 2) * width
            tile_turned[b // 2, k * width:(k + 1) * width, side:side + width] = tile_buf[b, k].T
    arrived_all(halo.at[0], halo_recv.at[0])
    for d in range(4):
        near[d] = halo[0, d]

    for it in range(ITERS):
        last = it == ITERS - 1
        if it:
            place(CENTRE, residual)
        for d in range(4):
            place(PLACES[d], near[d])
        coupled = []
        for b in range(0, blocks, 2):
            picked = jnp.concatenate([
                jnp.concatenate([ext[ids_ref[b + s, k]] for k in range(count)], axis=1) for s in range(2)
            ], axis=0)
            pair = jnp.dot(picked.astype(BF16), tile_turned[b // 2], preferred_element_type=F32)
            coupled += [pair[0:8, 0:width], pair[8:16, width:2 * width]]

        square = functools.reduce(jnp.add, chunks(residual * residual))
        sums = [
            jnp.sum(square, axis=0, keepdims=True),
            total([drag * square] + [c * c for c in coupled]),
        ]
        if it:
            mixed = functools.reduce(jnp.add, chunks(residual * direction))
            sums.append(total([drag * mixed] + [c * t for c, t in zip(coupled, track)]))
        else:
            sums.append(jnp.zeros((1, 128), F32))
        packed = jnp.zeros((1, 128), F32)
        for n, row in enumerate(sums):
            packed = jnp.where(lane == n, jnp.sum(row, axis=1, keepdims=True), packed)
        parts[it, me] = packed
        if last:
            each_peer(lambda step: sum_copy(it, step).start())

        for b in range(0, blocks, 2):
            blank = jnp.zeros((8, width), F32)
            diagonal = jnp.concatenate([
                jnp.concatenate([coupled[b], blank], axis=1),
                jnp.concatenate([blank, coupled[b + 1]], axis=1),
            ], axis=0)
            both = jnp.concatenate([tile_row(b), tile_row(b + 1)], axis=0)
            back = jnp.dot(diagonal.astype(BF16), both, preferred_element_type=F32)
            for k in range(count):
                spread[pl.ds((b * count + k) * 8, 8), :] = back[0:8, k * width:(k + 1) * width]
                spread[pl.ds(((b + 1) * count + k) * 8, 8), :] = back[8:16, k * width:(k + 1) * width]
        listed_spread = jnp.concatenate([spread[pl.ds(c, pairs, 8), :] for c in range(3)], axis=1)
        high = listed_spread.astype(BF16)
        low = (listed_spread - high.astype(F32)).astype(BF16)
        ret_out[it] = jnp.dot(
            selector, jnp.concatenate([high, low], axis=0), preferred_element_type=F32
        )
        for d in range(4):
            guarded(d, lambda d=d: ret_copy(it, d).start())
        if not last:
            each_peer(lambda step: sum_copy(it, step).start())

        if last:
            gathered = [0.0] * 9
            for d in (1, 2):
                guarded(d, lambda d=d: wait_for(rows_in.at[d], rows_recv.at[d]))
                rows = rows_in[d]
                fields = [near_velocity[d], near[d], near_direction[d]]
                stack = jnp.concatenate([part for f in fields for part in chunks(f)], axis=0)
                first = stack.astype(BF16)
                rest = stack - first.astype(F32)
                second = rest.astype(BF16)
                third = (rest - second.astype(F32)).astype(BF16)
                bead = lax.broadcasted_iota(jnp.int32, (width, 128), 0)
                onehot = jnp.where(bead == (rows & (width - 1)), 1.0, 0.0).astype(BF16)
                found = sum(
                    jnp.dot(piece, onehot, preferred_element_type=F32) for piece in (third, second, first)
                )
                block = lax.broadcasted_iota(jnp.int32, (blocks, 128), 0)
                mine = block == (rows >> (width.bit_length() - 1))
                for n in range(9):
                    part = jnp.where(mine, found[n * blocks:(n + 1) * blocks], 0.0)
                    gathered[n] = gathered[n] + jnp.sum(part, axis=0, keepdims=True)

        arrived_all(ret_in.at[it], ret_recv.at[it])
        product = drag3 * residual + ret_out[it, CENTRE * blocks:(CENTRE + 1) * blocks]
        for d in range(4):
            product = product + ret_in[it, d]
        if not last:
            own[it + 1] = product
            for d in range(4):
                guarded(d, lambda d=d: halo_copy(it + 1, d).start())

        wait_for(parts.at[it, pl.ds(0, everyone - 1)], sum_recv.at[it])
        summed = jnp.sum(parts[it], axis=0)
        norm, energy, cross = [
            jnp.sum(jnp.where(lane == n, summed, 0.0), axis=1, keepdims=True) for n in range(3)
        ]
        if it:
            beta = norm / norm_before
            energy = energy + 2.0 * beta * cross + beta * beta * energy_before
        alpha = norm / energy
        norm_before, energy_before = norm, energy

        def follow(now, before):
            return now + beta * before if it else now

        image = follow(product, image)
        direction = follow(residual, direction)
        velocity = velocity + alpha * direction if it else alpha * direction
        residual = residual - alpha * image
        if last:
            break
        track = [follow(c, t) for c, t in zip(coupled, track)]
        arrived_all(halo.at[it + 1], halo_recv.at[it + 1])
        for d in range(4):
            near_image[d] = follow(halo[it + 1, d], near_image[d])
            if d in (1, 2):
                near_direction[d] = follow(near[d], near_direction[d])
                step_v = alpha * near_direction[d]
                near_velocity[d] = near_velocity[d] + step_v if it else step_v
            near[d] = near[d] - alpha * near_image[d]

    for c in range(3):
        vel_ref[c] = chunks(velocity)[c]
        res_ref[c] = chunks(residual)[c]
    for c in range(3):
        row = gathered[c] + alpha * (gathered[3 + c] + beta * gathered[6 + c])
        arr_ref[c] = pltpu.roll(row, 64, 1)

    for d in (1, 2):
        guarded(d, lambda d=d: wait_for(rows_out.at[d], rows_send.at[d]))
    for d in range(4):
        guarded(d, lambda d=d: wait_for(own, halo_send.at[d]))
        guarded(d, lambda d=d: wait_for(own, ret_send.at[d]))
    wait_for(parts.at[:, pl.ds(0, everyone - 1)], sum_send)


def write_out(vel_in, res_in, arr_in, vel_ref, res_ref, arr_ref, sem):
    moves = ((vel_in, vel_ref), (res_in, res_ref), (arr_in, arr_ref))
    copies = [pltpu.make_async_copy(a, b, sem.at[n]) for n, (a, b) in enumerate(moves)]
    for copy in copies:
        copy.start()
    for copy in copies:
        copy.wait()


def on_device(n_ax, n_cr, force, self_drag, tiles, tile_ids, mig_rows, mig_count):
    blocks, width = force.shape[2], force.shape[4]
    count = tiles.shape[3]
    field = (blocks, 3 * width)
    vmem = pl.BlockSpec(memory_space=pltpu.VMEM)
    dma = pltpu.SemaphoreType.DMA
    hbm = pl.BlockSpec(memory_space=pltpu.HBM)
    solved = pl.pallas_call(
        functools.partial(kernel, n_ax, n_cr),
        out_shape=(
            pltpu.VMEM((3, blocks, width), F32),
            pltpu.VMEM((3, blocks, width), F32),
            pltpu.VMEM((3, 1, 2 * mig_rows.shape[3]), F32),
        ),
        in_specs=[hbm] * 6,
        out_specs=(vmem, vmem, vmem),
        scratch_shapes=[
            pltpu.SMEM((blocks, count), jnp.int32),
            pltpu.SMEM((2,), jnp.int32),
            pltpu.VMEM((3, blocks, width), F32),
            pltpu.VMEM((blocks, width), F32),
            pltpu.VMEM(mig_rows.shape[2:], jnp.int32),
            pltpu.VMEM((blocks, count, width, width), BF16),
            pltpu.VMEM((blocks // 2, count * width, 2 * width), BF16),
            pltpu.VMEM((8 * blocks, 8, width), F32),
            pltpu.VMEM((blocks * count * 8, width), F32),
            pltpu.VMEM((ITERS,) + field, F32),
            pltpu.VMEM((ITERS, 4) + field, F32),
            pltpu.VMEM((ITERS, 8 * blocks, 3 * width), F32),
            pltpu.VMEM((ITERS, 4) + field, F32),
            pltpu.VMEM((ITERS, n_ax * n_cr, 1, 128), F32),
            pltpu.VMEM((8, 128), jnp.int32),
            pltpu.VMEM((3, 1, 128), jnp.int32),
            pltpu.VMEM((3, 1, 128), jnp.int32),
            dma, dma((5,)),
            dma((4,)), dma((ITERS,)),
            dma((4,)), dma((ITERS,)),
            dma((3,)), dma((3,)),
            dma, dma((ITERS,)),
        ],
        compiler_params=pltpu.CompilerParams(
            collective_id=0, has_side_effects=True, vmem_limit_bytes=60 * 1024 * 1024
        ),
        name="cg_solve",
    )(
        tile_ids.reshape(tile_ids.shape[2:]),
        mig_count.reshape(mig_count.shape[2:]),
        jnp.swapaxes(force[0, 0], 0, 1),
        self_drag.reshape(self_drag.shape[2:]),
        tiles.reshape(tiles.shape[2:]),
        mig_rows.reshape(mig_rows.shape[2:]),
    )
    velocity, residual, arrivals = pl.pallas_call(
        write_out,
        out_shape=tuple(jax.ShapeDtypeStruct(x.shape, x.dtype) for x in solved),
        in_specs=[vmem] * 3,
        out_specs=(hbm,) * 3,
        scratch_shapes=[dma((3,))],
        compiler_params=pltpu.CompilerParams(vmem_limit_bytes=1024 * 1024),
        name="write_out",
    )(*solved)
    velocity, residual = jnp.swapaxes(velocity, 0, 1), jnp.swapaxes(residual, 0, 1)
    return velocity[None, None], residual[None, None], arrivals[:, 0][None, None]


def solution(mesh):
    placed = (
        P("axial", "cross", None, None, None),
        P("axial", "cross", None, None),
        P("axial", "cross", None, None, None, None),
        P("axial", "cross", None, None),
        P("axial", "cross", None, None),
        P("axial", "cross", None),
    )
    return jax.shard_map(
        functools.partial(on_device, mesh.shape["axial"], mesh.shape["cross"]),
        mesh=mesh,
        in_specs=placed,
        out_specs=(
            P("axial", "cross", None, None, None),
            P("axial", "cross", None, None, None),
            P("axial", "cross", None, None),
        ),
        check_vma=False,
    )
```

```python
import functools

import jax
import jax.numpy as jnp
from jax import lax
from jax.experimental import pallas as pl
from jax.experimental.pallas import tpu as pltpu
from jax.sharding import PartitionSpec as P

ITERS = 3
LOGICAL = pl.DeviceIdType.LOGICAL
PLACES = (1, 3, 5, 7)
CENTRE = 4
F32 = jnp.float32
BF16 = jnp.bfloat16


def chunks(field):
    return [field[:, c * 128:(c + 1) * 128] for c in range(3)]


def kernel(
    n_ax, n_cr,
    ids_hbm, count_hbm, force_hbm, drag_hbm, tiles_ref, rows_hbm,
    vel_ref, res_ref, arr_ref,
    ids_ref, count_ref, force_ref, drag_ref, rows_ref, tile_buf, tile_turned, ext, spread, own, halo, ret_out, ret_in, parts, mig, rows_out, rows_in,
    tile_sem, small_sem, halo_send, halo_recv, ret_send, ret_recv, rows_send, rows_recv,
    sum_send, sum_recv,
):
    blocks, count, width = tiles_ref.shape[0], tiles_ref.shape[1], tiles_ref.shape[2]
    pairs = blocks * count
    slot = rows_hbm.shape[1]
    me_a = lax.axis_index("axial")
    me_c = lax.axis_index("cross")

    me = me_a * n_cr + me_c
    device = (
        jnp.where(me_a > 0, me - n_cr, me + (n_ax - 1) * n_cr),
        me - 1,
        me + 1,
        jnp.where(me_a + 1 < n_ax, me + n_cr, me - (n_ax - 1) * n_cr),
    )
    exists = (None, me_c > 0, me_c + 1 < n_cr, None)

    def guarded(d, act):
        if exists[d] is None:
            act()
        else:
            pl.when(exists[d])(act)

    def neighbour(src, dst, send, recv, d):
        return pltpu.make_async_remote_copy(
            src_ref=src, dst_ref=dst.at[3 - d], send_sem=send, recv_sem=recv,
            device_id=device[d], device_id_type=LOGICAL,
        )

    def halo_copy(stage, d):
        return neighbour(own.at[stage], halo.at[stage], halo_send.at[d], halo_recv.at[stage], d)

    def ret_copy(it, d):
        src = ret_out.at[it, pl.ds(PLACES[d] * blocks, blocks)]
        return neighbour(src, ret_in.at[it], ret_send.at[d], ret_recv.at[it], d)

    def rows_copy(d):
        return neighbour(rows_out.at[d], rows_in, rows_send.at[d], rows_recv.at[3 - d], d)

    def wait_for(ref, sem):
        pltpu.make_async_copy(ref, ref, sem).wait()

    inner = exists[1] & exists[2]

    def arrived_all(ref, sem):
        @pl.when(inner)
        def _():
            wait_for(ref, sem)

        @pl.when(jnp.logical_not(inner))
        def _():
            wait_for(ref.at[pl.ds(0, 3)], sem)

    everyone = n_ax * n_cr

    def peer(step):
        return jnp.where(me + step < everyone, me + step, me + step - everyone)

    def sum_copy(it, step):
        return pltpu.make_async_remote_copy(
            src_ref=parts.at[it, me], dst_ref=parts.at[it, me],
            send_sem=sum_send, recv_sem=sum_recv.at[it],
            device_id=peer(step), device_id_type=LOGICAL,
        )

    def each_peer(act):
        def body(step, carry):
            act(step)
            return carry
        if everyone > 64:
            lax.fori_loop(1, everyone, body, 0)
        else:
            for step in range(1, everyone):
                act(step)

    fetched = (
        (force_hbm, force_ref), (ids_hbm, ids_ref), (count_hbm, count_ref),
        (drag_hbm, drag_ref), (rows_hbm, rows_ref),
    )
    small = [pltpu.make_async_copy(a, b, small_sem.at[n]) for n, (a, b) in enumerate(fetched)]
    small[0].start()

    barrier = pltpu.get_barrier_semaphore()
    each_peer(lambda step: pl.semaphore_signal(barrier, inc=1, device_id=peer(step), device_id_type=LOGICAL))

    for copy in small[1:]:
        copy.start()
    load = pltpu.make_async_copy(tiles_ref, tile_buf, tile_sem)
    load.start()
    for copy in small:
        copy.wait()

    force = jnp.concatenate([force_ref[c] for c in range(3)], axis=1)
    own[0] = force
    lane = lax.broadcasted_iota(jnp.int32, (1, 128), 1)
    mig[0:2, 0:slot] = rows_ref[...]
    listed = mig[...]
    turned = pltpu.roll(listed, 64, 1)
    rows_out[1] = jnp.where((lane < slot) & (lane < count_ref[0]), listed[0:1], -1)
    rows_out[2] = jnp.where((lane >= 64) & (lane - 64 < count_ref[1]), turned[1:2], -1)

    for d in (1, 2):
        @pl.when(jnp.logical_not(exists[d]))
        def _():
            for stage in range(ITERS):
                halo[stage, d] = jnp.zeros((blocks, 3 * width), F32)
                ret_in[stage, d] = jnp.zeros((blocks, 3 * width), F32)
            rows_in[d] = jnp.full((1, 128), -1, jnp.int32)

    pl.semaphore_wait(barrier, everyone - 1)

    for d in range(4):
        guarded(d, lambda d=d: halo_copy(0, d).start())
    for d in (1, 2):
        guarded(d, lambda d=d: rows_copy(d).start())

    ext[...] = jnp.zeros(ext.shape, F32)
    wide = lax.broadcasted_iota(jnp.int32, (1, 2 * pairs), 1)
    listed_ids = jnp.zeros((1, 2 * pairs), jnp.int32)
    for n in range(pairs):
        hit = (wide == n) | (wide == n + pairs)
        listed_ids = jnp.where(hit, ids_ref[n // count, n % count], listed_ids)
    entry = lax.broadcasted_iota(jnp.int32, (8 * blocks, 2 * pairs), 0)
    selector = jnp.where(entry == listed_ids, 1.0, 0.0).astype(BF16)
    drag = drag_ref[...]
    drag3 = jnp.concatenate([drag] * 3, axis=1)

    def place(p, field):
        for c, part in enumerate(chunks(field)):
            ext[p * blocks:(p + 1) * blocks, c, :] = part

    def tile_row(b):
        return jnp.concatenate([tile_buf[b, k] for k in range(count)], axis=1)

    def total(parts):
        return jnp.sum(functools.reduce(jnp.add, parts), axis=0, keepdims=True)

    place(CENTRE, force)
    residual = force
    velocity = direction = image = None
    near = [None] * 4
    near_image = [None] * 4
    near_velocity = [None] * 4
    near_direction = [None] * 4
    track = [None] * blocks
    norm_before = energy_before = None

    load.wait()
    for b in range(blocks):
        for k in range(count):
            side = (b % 2) * width
            tile_turned[b // 2, k * width:(k + 1) * width, side:side + width] = tile_buf[b, k].T
    arrived_all(halo.at[0], halo_recv.at[0])
    for d in range(4):
        near[d] = halo[0, d]

    for it in range(ITERS):
        last = it == ITERS - 1
        if it:
            place(CENTRE, residual)
        for d in range(4):
            place(PLACES[d], near[d])
        coupled = []
        for b in range(0, blocks, 2):
            picked = jnp.concatenate([
                jnp.concatenate([ext[ids_ref[b + s, k]] for k in range(count)], axis=1) for s in range(2)
            ], axis=0)
            pair = jnp.dot(picked.astype(BF16), tile_turned[b // 2], preferred_element_type=F32)
            coupled += [pair[0:8, 0:width], pair[8:16, width:2 * width]]

        square = functools.reduce(jnp.add, chunks(residual * residual))
        sums = [
            jnp.sum(square, axis=0, keepdims=True),
            total([drag * square] + [c * c for c in coupled]),
        ]
        if it:
            mixed = functools.reduce(jnp.add, chunks(residual * direction))
            sums.append(total([drag * mixed] + [c * t for c, t in zip(coupled, track)]))
        else:
            sums.append(jnp.zeros((1, 128), F32))
        packed = jnp.zeros((1, 128), F32)
        for n, row in enumerate(sums):
            packed = jnp.where(lane == n, jnp.sum(row, axis=1, keepdims=True), packed)
        parts[it, me] = packed
        if last:
            each_peer(lambda step: sum_copy(it, step).start())

        for b in range(0, blocks, 2):
            blank = jnp.zeros((8, width), F32)
            diagonal = jnp.concatenate([
                jnp.concatenate([coupled[b], blank], axis=1),
                jnp.concatenate([blank, coupled[b + 1]], axis=1),
            ], axis=0)
            both = jnp.concatenate([tile_row(b), tile_row(b + 1)], axis=0)
            back = jnp.dot(diagonal.astype(BF16), both, preferred_element_type=F32)
            for k in range(count):
                spread[pl.ds((b * count + k) * 8, 8), :] = back[0:8, k * width:(k + 1) * width]
                spread[pl.ds(((b + 1) * count + k) * 8, 8), :] = back[8:16, k * width:(k + 1) * width]
        listed_spread = jnp.concatenate([spread[pl.ds(c, pairs, 8), :] for c in range(3)], axis=1)
        high = listed_spread.astype(BF16)
        low = (listed_spread - high.astype(F32)).astype(BF16)
        ret_out[it] = jnp.dot(
            selector, jnp.concatenate([high, low], axis=0), preferred_element_type=F32
        )
        for d in range(4):
            guarded(d, lambda d=d: ret_copy(it, d).start())
        if not last:
            each_peer(lambda step: sum_copy(it, step).start())

        if last:
            gathered = [0.0] * 9
            for d in (1, 2):
                guarded(d, lambda d=d: wait_for(rows_in.at[d], rows_recv.at[d]))
                rows = rows_in[d]
                fields = [near_velocity[d], near[d], near_direction[d]]
                stack = jnp.concatenate([part for f in fields for part in chunks(f)], axis=0)
                first = stack.astype(BF16)
                rest = stack - first.astype(F32)
                second = rest.astype(BF16)
                third = (rest - second.astype(F32)).astype(BF16)
                bead = lax.broadcasted_iota(jnp.int32, (width, 128), 0)
                onehot = jnp.where(bead == (rows & (width - 1)), 1.0, 0.0).astype(BF16)
                found = sum(
                    jnp.dot(piece, onehot, preferred_element_type=F32) for piece in (third, second, first)
                )
                block = lax.broadcasted_iota(jnp.int32, (blocks, 128), 0)
                mine = block == (rows >> (width.bit_length() - 1))
                for n in range(9):
                    part = jnp.where(mine, found[n * blocks:(n + 1) * blocks], 0.0)
                    gathered[n] = gathered[n] + jnp.sum(part, axis=0, keepdims=True)

        arrived_all(ret_in.at[it], ret_recv.at[it])
        product = drag3 * residual + ret_out[it, CENTRE * blocks:(CENTRE + 1) * blocks]
        for d in range(4):
            product = product + ret_in[it, d]
        if not last:
            own[it + 1] = product
            for d in range(4):
                guarded(d, lambda d=d: halo_copy(it + 1, d).start())

        wait_for(parts.at[it, pl.ds(0, everyone - 1)], sum_recv.at[it])
        summed = jnp.sum(parts[it], axis=0)
        norm, energy, cross = [
            jnp.sum(jnp.where(lane == n, summed, 0.0), axis=1, keepdims=True) for n in range(3)
        ]
        if it:
            beta = norm / norm_before
            energy = energy + 2.0 * beta * cross + beta * beta * energy_before
        alpha = norm / energy
        norm_before, energy_before = norm, energy

        def follow(now, before):
            return now + beta * before if it else now

        image = follow(product, image)
        direction = follow(residual, direction)
        velocity = velocity + alpha * direction if it else alpha * direction
        residual = residual - alpha * image
        if last:
            break
        track = [follow(c, t) for c, t in zip(coupled, track)]
        arrived_all(halo.at[it + 1], halo_recv.at[it + 1])
        for d in range(4):
            near_image[d] = follow(halo[it + 1, d], near_image[d])
            if d in (1, 2):
                near_direction[d] = follow(near[d], near_direction[d])
                step_v = alpha * near_direction[d]
                near_velocity[d] = near_velocity[d] + step_v if it else step_v
            near[d] = near[d] - alpha * near_image[d]

    for c in range(3):
        vel_ref[c] = chunks(velocity)[c]
        res_ref[c] = chunks(residual)[c]
    for c in range(3):
        row = gathered[c] + alpha * (gathered[3 + c] + beta * gathered[6 + c])
        arr_ref[c] = pltpu.roll(row, 64, 1)

    for d in (1, 2):
        guarded(d, lambda d=d: wait_for(rows_out.at[d], rows_send.at[d]))
    for d in range(4):
        guarded(d, lambda d=d: wait_for(own, halo_send.at[d]))
        guarded(d, lambda d=d: wait_for(own, ret_send.at[d]))
    wait_for(parts.at[:, pl.ds(0, everyone - 1)], sum_send)


def write_out(vel_in, res_in, arr_in, vel_ref, res_ref, arr_ref, sem):
    moves = ((vel_in, vel_ref), (res_in, res_ref), (arr_in, arr_ref))
    copies = [pltpu.make_async_copy(a, b, sem.at[n]) for n, (a, b) in enumerate(moves)]
    for copy in copies:
        copy.start()
    for copy in copies:
        copy.wait()


def on_device(n_ax, n_cr, force, self_drag, tiles, tile_ids, mig_rows, mig_count):
    blocks, width = force.shape[2], force.shape[4]
    count = tiles.shape[3]
    field = (blocks, 3 * width)
    vmem = pl.BlockSpec(memory_space=pltpu.VMEM)
    dma = pltpu.SemaphoreType.DMA
    hbm = pl.BlockSpec(memory_space=pltpu.HBM)
    solved = pl.pallas_call(
        functools.partial(kernel, n_ax, n_cr),
        out_shape=(
            pltpu.VMEM((3, blocks, width), F32),
            pltpu.VMEM((3, blocks, width), F32),
            pltpu.VMEM((3, 1, 2 * mig_rows.shape[3]), F32),
        ),
        in_specs=[hbm] * 6,
        out_specs=(vmem, vmem, vmem),
        scratch_shapes=[
            pltpu.SMEM((blocks, count), jnp.int32),
            pltpu.SMEM((2,), jnp.int32),
            pltpu.VMEM((3, blocks, width), F32),
            pltpu.VMEM((blocks, width), F32),
            pltpu.VMEM(mig_rows.shape[2:], jnp.int32),
            pltpu.VMEM((blocks, count, width, width), BF16),
            pltpu.VMEM((blocks // 2, count * width, 2 * width), BF16),
            pltpu.VMEM((8 * blocks, 8, width), F32),
            pltpu.VMEM((blocks * count * 8, width), F32),
            pltpu.VMEM((ITERS,) + field, F32),
            pltpu.VMEM((ITERS, 4) + field, F32),
            pltpu.VMEM((ITERS, 8 * blocks, 3 * width), F32),
            pltpu.VMEM((ITERS, 4) + field, F32),
            pltpu.VMEM((ITERS, n_ax * n_cr, 1, 128), F32),
            pltpu.VMEM((8, 128), jnp.int32),
            pltpu.VMEM((3, 1, 128), jnp.int32),
            pltpu.VMEM((3, 1, 128), jnp.int32),
            dma, dma((5,)),
            dma((4,)), dma((ITERS,)),
            dma((4,)), dma((ITERS,)),
            dma((3,)), dma((3,)),
            dma, dma((ITERS,)),
        ],
        compiler_params=pltpu.CompilerParams(
            collective_id=0, has_side_effects=True, vmem_limit_bytes=60 * 1024 * 1024
        ),
        name="cg_solve",
    )(
        tile_ids.reshape(tile_ids.shape[2:]),
        mig_count.reshape(mig_count.shape[2:]),
        jnp.swapaxes(force[0, 0], 0, 1),
        self_drag.reshape(self_drag.shape[2:]),
        tiles.reshape(tiles.shape[2:]),
        mig_rows.reshape(mig_rows.shape[2:]),
    )
    velocity, residual, arrivals = pl.pallas_call(
        write_out,
        out_shape=tuple(jax.ShapeDtypeStruct(x.shape, x.dtype) for x in solved),
        in_specs=[vmem] * 3,
        out_specs=(hbm,) * 3,
        scratch_shapes=[dma((3,))],
        compiler_params=pltpu.CompilerParams(vmem_limit_bytes=1024 * 1024),
        name="write_out",
    )(*solved)
    velocity, residual = jnp.swapaxes(velocity, 0, 1), jnp.swapaxes(residual, 0, 1)
    return velocity[None, None], residual[None, None], arrivals[:, 0][None, None]


def solution(mesh):
    placed = (
        P("axial", "cross", None, None, None),
        P("axial", "cross", None, None),
        P("axial", "cross", None, None, None, None),
        P("axial", "cross", None, None),
        P("axial", "cross", None, None),
        P("axial", "cross", None),
    )
    return jax.shard_map(
        functools.partial(on_device, mesh.shape["axial"], mesh.shape["cross"]),
        mesh=mesh,
        in_specs=placed,
        out_specs=(
            P("axial", "cross", None, None, None),
            P("axial", "cross", None, None, None),
            P("axial", "cross", None, None),
        ),
        check_vma=False,
    )
```

```python
import functools

import jax
import jax.numpy as jnp
from jax import lax
from jax.experimental import pallas as pl
from jax.experimental.pallas import tpu as pltpu
from jax.sharding import PartitionSpec as P

ITERS = 3
LOGICAL = pl.DeviceIdType.LOGICAL
PLACES = (1, 3, 5, 7)
CENTRE = 4
F32 = jnp.float32
BF16 = jnp.bfloat16


def chunks(field):
    return [field[:, c * 128:(c + 1) * 128] for c in range(3)]


def kernel(
    n_ax, n_cr,
    ids_hbm, count_hbm, force_hbm, drag_hbm, tiles_ref, rows_hbm,
    vel_ref, res_ref, arr_ref,
    ids_ref, count_ref, force_ref, drag_ref, rows_ref, tile_buf, tile_turned, ext, spread, own, halo, ret_out, ret_in, parts, mig, rows_out, rows_in,
    tile_sem, small_sem, halo_send, halo_recv, ret_send, ret_recv, rows_send, rows_recv,
    sum_send, sum_recv,
):
    blocks, count, width = tiles_ref.shape[0], tiles_ref.shape[1], tiles_ref.shape[2]
    pairs = blocks * count
    slot = rows_hbm.shape[1]
    me_a = lax.axis_index("axial")
    me_c = lax.axis_index("cross")

    me = me_a * n_cr + me_c
    device = (
        jnp.where(me_a > 0, me - n_cr, me + (n_ax - 1) * n_cr),
        me - 1,
        me + 1,
        jnp.where(me_a + 1 < n_ax, me + n_cr, me - (n_ax - 1) * n_cr),
    )
    exists = (None, me_c > 0, me_c + 1 < n_cr, None)

    def guarded(d, act):
        if exists[d] is None:
            act()
        else:
            pl.when(exists[d])(act)

    def neighbour(src, dst, send, recv, d):
        return pltpu.make_async_remote_copy(
            src_ref=src, dst_ref=dst.at[3 - d], send_sem=send, recv_sem=recv,
            device_id=device[d], device_id_type=LOGICAL,
        )

    def halo_copy(stage, d):
        return neighbour(own.at[stage], halo.at[stage], halo_send.at[d], halo_recv.at[stage], d)

    def ret_copy(it, d):
        src = ret_out.at[it, pl.ds(PLACES[d] * blocks, blocks)]
        return neighbour(src, ret_in.at[it], ret_send.at[d], ret_recv.at[it], d)

    def rows_copy(d):
        return neighbour(rows_out.at[d], rows_in, rows_send.at[d], rows_recv.at[3 - d], d)

    def wait_for(ref, sem):
        pltpu.make_async_copy(ref, ref, sem).wait()

    inner = exists[1] & exists[2]

    def arrived_all(ref, sem):
        @pl.when(inner)
        def _():
            wait_for(ref, sem)

        @pl.when(jnp.logical_not(inner))
        def _():
            wait_for(ref.at[pl.ds(0, 3)], sem)

    everyone = n_ax * n_cr

    def peer(step):
        return jnp.where(me + step < everyone, me + step, me + step - everyone)

    def sum_copy(it, step):
        return pltpu.make_async_remote_copy(
            src_ref=parts.at[it, me], dst_ref=parts.at[it, me],
            send_sem=sum_send, recv_sem=sum_recv.at[it],
            device_id=peer(step), device_id_type=LOGICAL,
        )

    def each_peer(act):
        def body(step, carry):
            act(step)
            return carry
        if everyone > 64:
            lax.fori_loop(1, everyone, body, 0)
        else:
            for step in range(1, everyone):
                act(step)

    fetched = (
        (force_hbm, force_ref), (ids_hbm, ids_ref), (count_hbm, count_ref),
        (drag_hbm, drag_ref), (rows_hbm, rows_ref),
    )
    small = [pltpu.make_async_copy(a, b, small_sem.at[n]) for n, (a, b) in enumerate(fetched)]
    small[0].start()

    barrier = pltpu.get_barrier_semaphore()
    each_peer(lambda step: pl.semaphore_signal(barrier, inc=1, device_id=peer(step), device_id_type=LOGICAL))

    for copy in small[1:]:
        copy.start()
    load = pltpu.make_async_copy(tiles_ref, tile_buf, tile_sem)
    load.start()
    for copy in small:
        copy.wait()

    force = jnp.concatenate([force_ref[c] for c in range(3)], axis=1)
    own[0] = force
    lane = lax.broadcasted_iota(jnp.int32, (1, 128), 1)
    mig[0:2, 0:slot] = rows_ref[...]
    listed = mig[...]
    turned = pltpu.roll(listed, 64, 1)
    rows_out[1] = jnp.where((lane < slot) & (lane < count_ref[0]), listed[0:1], -1)
    rows_out[2] = jnp.where((lane >= 64) & (lane - 64 < count_ref[1]), turned[1:2], -1)

    for d in (1, 2):
        @pl.when(jnp.logical_not(exists[d]))
        def _():
            for stage in range(ITERS):
                halo[stage, d] = jnp.zeros((blocks, 3 * width), F32)
                ret_in[stage, d] = jnp.zeros((blocks, 3 * width), F32)
            rows_in[d] = jnp.full((1, 128), -1, jnp.int32)

    pl.semaphore_wait(barrier, everyone - 1)

    for d in range(4):
        guarded(d, lambda d=d: halo_copy(0, d).start())
    for d in (1, 2):
        guarded(d, lambda d=d: rows_copy(d).start())

    ext[...] = jnp.zeros(ext.shape, F32)
    wide = lax.broadcasted_iota(jnp.int32, (1, 2 * pairs), 1)
    listed_ids = jnp.zeros((1, 2 * pairs), jnp.int32)
    for n in range(pairs):
        hit = (wide == n) | (wide == n + pairs)
        listed_ids = jnp.where(hit, ids_ref[n // count, n % count], listed_ids)
    entry = lax.broadcasted_iota(jnp.int32, (8 * blocks, 2 * pairs), 0)
    selector = jnp.where(entry == listed_ids, 1.0, 0.0).astype(BF16)
    drag = drag_ref[...]
    drag3 = jnp.concatenate([drag] * 3, axis=1)

    def place(p, field):
        for c, part in enumerate(chunks(field)):
            ext[p * blocks:(p + 1) * blocks, c, :] = part

    def tile_row(b):
        return jnp.concatenate([tile_buf[b, k] for k in range(count)], axis=1)

    def total(parts):
        return jnp.sum(functools.reduce(jnp.add, parts), axis=0, keepdims=True)

    place(CENTRE, force)
    residual = force
    velocity = direction = image = None
    near = [None] * 4
    near_image = [None] * 4
    near_velocity = [None] * 4
    near_direction = [None] * 4
    track = [None] * blocks
    norm_before = energy_before = None

    load.wait()
    for b in range(blocks):
        for k in range(count):
            side = (b % 2) * width
            tile_turned[b // 2, k * width:(k + 1) * width, side:side + width] = tile_buf[b, k].T
    arrived_all(halo.at[0], halo_recv.at[0])
    for d in range(4):
        near[d] = halo[0, d]

    for it in range(ITERS):
        last = it == ITERS - 1
        if it:
            place(CENTRE, residual)
        for d in range(4):
            place(PLACES[d], near[d])
        coupled = []
        for b in range(0, blocks, 2):
            picked = jnp.concatenate([
                jnp.concatenate([ext[ids_ref[b + s, k]] for k in range(count)], axis=1) for s in range(2)
            ], axis=0)
            pair = jnp.dot(picked.astype(BF16), tile_turned[b // 2], preferred_element_type=F32)
            coupled += [pair[0:8, 0:width], pair[8:16, width:2 * width]]

        square = functools.reduce(jnp.add, chunks(residual * residual))
        sums = [
            jnp.sum(square, axis=0, keepdims=True),
            total([drag * square] + [c * c for c in coupled]),
        ]
        if it:
            mixed = functools.reduce(jnp.add, chunks(residual * direction))
            sums.append(total([drag * mixed] + [c * t for c, t in zip(coupled, track)]))
        else:
            sums.append(jnp.zeros((1, 128), F32))
        packed = jnp.zeros((1, 128), F32)
        for n, row in enumerate(sums):
            packed = jnp.where(lane == n, jnp.sum(row, axis=1, keepdims=True), packed)
        parts[it, me] = packed
        for b in range(0, blocks, 2):
            blank = jnp.zeros((8, width), F32)
            diagonal = jnp.concatenate([
                jnp.concatenate([coupled[b], blank], axis=1),
                jnp.concatenate([blank, coupled[b + 1]], axis=1),
            ], axis=0)
            both = jnp.concatenate([tile_row(b), tile_row(b + 1)], axis=0)
            back = jnp.dot(diagonal.astype(BF16), both, preferred_element_type=F32)
            for k in range(count):
                spread[pl.ds((b * count + k) * 8, 8), :] = back[0:8, k * width:(k + 1) * width]
                spread[pl.ds(((b + 1) * count + k) * 8, 8), :] = back[8:16, k * width:(k + 1) * width]
        listed_spread = jnp.concatenate([spread[pl.ds(c, pairs, 8), :] for c in range(3)], axis=1)
        high = listed_spread.astype(BF16)
        low = (listed_spread - high.astype(F32)).astype(BF16)
        ret_out[it] = jnp.dot(
            selector, jnp.concatenate([high, low], axis=0), preferred_element_type=F32
        )
        for d in range(4):
            guarded(d, lambda d=d: ret_copy(it, d).start())
        each_peer(lambda step: sum_copy(it, step).start())

        if last:
            gathered = [0.0] * 9
            for d in (1, 2):
                guarded(d, lambda d=d: wait_for(rows_in.at[d], rows_recv.at[d]))
                rows = rows_in[d]
                fields = [near_velocity[d], near[d], near_direction[d]]
                stack = jnp.concatenate([part for f in fields for part in chunks(f)], axis=0)
                first = stack.astype(BF16)
                rest = stack - first.astype(F32)
                second = rest.astype(BF16)
                third = (rest - second.astype(F32)).astype(BF16)
                bead = lax.broadcasted_iota(jnp.int32, (width, 128), 0)
                onehot = jnp.where(bead == (rows & (width - 1)), 1.0, 0.0).astype(BF16)
                found = sum(
                    jnp.dot(piece, onehot, preferred_element_type=F32) for piece in (third, second, first)
                )
                block = lax.broadcasted_iota(jnp.int32, (blocks, 128), 0)
                mine = block == (rows >> (width.bit_length() - 1))
                for n in range(9):
                    part = jnp.where(mine, found[n * blocks:(n + 1) * blocks], 0.0)
                    gathered[n] = gathered[n] + jnp.sum(part, axis=0, keepdims=True)

        arrived_all(ret_in.at[it], ret_recv.at[it])
        product = drag3 * residual + ret_out[it, CENTRE * blocks:(CENTRE + 1) * blocks]
        for d in range(4):
            product = product + ret_in[it, d]
        if not last:
            own[it + 1] = product
            for d in range(4):
                guarded(d, lambda d=d: halo_copy(it + 1, d).start())

        wait_for(parts.at[it, pl.ds(0, everyone - 1)], sum_recv.at[it])
        summed = jnp.sum(parts[it], axis=0)
        norm, energy, cross = [
            jnp.sum(jnp.where(lane == n, summed, 0.0), axis=1, keepdims=True) for n in range(3)
        ]
        if it:
            beta = norm / norm_before
            energy = energy + 2.0 * beta * cross + beta * beta * energy_before
        alpha = norm / energy
        norm_before, energy_before = norm, energy

        def follow(now, before):
            return now + beta * before if it else now

        image = follow(product, image)
        direction = follow(residual, direction)
        velocity = velocity + alpha * direction if it else alpha * direction
        residual = residual - alpha * image
        if last:
            break
        track = [follow(c, t) for c, t in zip(coupled, track)]
        arrived_all(halo.at[it + 1], halo_recv.at[it + 1])
        for d in range(4):
            near_image[d] = follow(halo[it + 1, d], near_image[d])
            if d in (1, 2):
                near_direction[d] = follow(near[d], near_direction[d])
                step_v = alpha * near_direction[d]
                near_velocity[d] = near_velocity[d] + step_v if it else step_v
            near[d] = near[d] - alpha * near_image[d]

    for c in range(3):
        vel_ref[c] = chunks(velocity)[c]
        res_ref[c] = chunks(residual)[c]
    for c in range(3):
        row = gathered[c] + alpha * (gathered[3 + c] + beta * gathered[6 + c])
        arr_ref[c] = pltpu.roll(row, 64, 1)

    for d in (1, 2):
        guarded(d, lambda d=d: wait_for(rows_out.at[d], rows_send.at[d]))
    for d in range(4):
        guarded(d, lambda d=d: wait_for(own, halo_send.at[d]))
        guarded(d, lambda d=d: wait_for(own, ret_send.at[d]))
    wait_for(parts.at[:, pl.ds(0, everyone - 1)], sum_send)


def write_out(vel_in, res_in, arr_in, vel_ref, res_ref, arr_ref, sem):
    moves = ((vel_in, vel_ref), (res_in, res_ref), (arr_in, arr_ref))
    copies = [pltpu.make_async_copy(a, b, sem.at[n]) for n, (a, b) in enumerate(moves)]
    for copy in copies:
        copy.start()
    for copy in copies:
        copy.wait()


def on_device(n_ax, n_cr, force, self_drag, tiles, tile_ids, mig_rows, mig_count):
    blocks, width = force.shape[2], force.shape[4]
    count = tiles.shape[3]
    field = (blocks, 3 * width)
    vmem = pl.BlockSpec(memory_space=pltpu.VMEM)
    dma = pltpu.SemaphoreType.DMA
    hbm = pl.BlockSpec(memory_space=pltpu.HBM)
    solved = pl.pallas_call(
        functools.partial(kernel, n_ax, n_cr),
        out_shape=(
            pltpu.VMEM((3, blocks, width), F32),
            pltpu.VMEM((3, blocks, width), F32),
            pltpu.VMEM((3, 1, 2 * mig_rows.shape[3]), F32),
        ),
        in_specs=[hbm] * 6,
        out_specs=(vmem, vmem, vmem),
        scratch_shapes=[
            pltpu.SMEM((blocks, count), jnp.int32),
            pltpu.SMEM((2,), jnp.int32),
            pltpu.VMEM((3, blocks, width), F32),
            pltpu.VMEM((blocks, width), F32),
            pltpu.VMEM(mig_rows.shape[2:], jnp.int32),
            pltpu.VMEM((blocks, count, width, width), BF16),
            pltpu.VMEM((blocks // 2, count * width, 2 * width), BF16),
            pltpu.VMEM((8 * blocks, 8, width), F32),
            pltpu.VMEM((blocks * count * 8, width), F32),
            pltpu.VMEM((ITERS,) + field, F32),
            pltpu.VMEM((ITERS, 4) + field, F32),
            pltpu.VMEM((ITERS, 8 * blocks, 3 * width), F32),
            pltpu.VMEM((ITERS, 4) + field, F32),
            pltpu.VMEM((ITERS, n_ax * n_cr, 1, 128), F32),
            pltpu.VMEM((8, 128), jnp.int32),
            pltpu.VMEM((3, 1, 128), jnp.int32),
            pltpu.VMEM((3, 1, 128), jnp.int32),
            dma, dma((5,)),
            dma((4,)), dma((ITERS,)),
            dma((4,)), dma((ITERS,)),
            dma((3,)), dma((3,)),
            dma, dma((ITERS,)),
        ],
        compiler_params=pltpu.CompilerParams(
            collective_id=0, has_side_effects=True, vmem_limit_bytes=60 * 1024 * 1024
        ),
        name="cg_solve",
    )(
        tile_ids.reshape(tile_ids.shape[2:]),
        mig_count.reshape(mig_count.shape[2:]),
        jnp.swapaxes(force[0, 0], 0, 1),
        self_drag.reshape(self_drag.shape[2:]),
        tiles.reshape(tiles.shape[2:]),
        mig_rows.reshape(mig_rows.shape[2:]),
    )
    velocity, residual, arrivals = pl.pallas_call(
        write_out,
        out_shape=tuple(jax.ShapeDtypeStruct(x.shape, x.dtype) for x in solved),
        in_specs=[vmem] * 3,
        out_specs=(hbm,) * 3,
        scratch_shapes=[dma((3,))],
        compiler_params=pltpu.CompilerParams(vmem_limit_bytes=1024 * 1024),
        name="write_out",
    )(*solved)
    velocity, residual = jnp.swapaxes(velocity, 0, 1), jnp.swapaxes(residual, 0, 1)
    return velocity[None, None], residual[None, None], arrivals[:, 0][None, None]


def solution(mesh):
    placed = (
        P("axial", "cross", None, None, None),
        P("axial", "cross", None, None),
        P("axial", "cross", None, None, None, None),
        P("axial", "cross", None, None),
        P("axial", "cross", None, None),
        P("axial", "cross", None),
    )
    return jax.shard_map(
        functools.partial(on_device, mesh.shape["axial"], mesh.shape["cross"]),
        mesh=mesh,
        in_specs=placed,
        out_specs=(
            P("axial", "cross", None, None, None),
            P("axial", "cross", None, None, None),
            P("axial", "cross", None, None),
        ),
        check_vma=False,
    )
```
